512 devices in a mesh: img: 16 (over x, y), tile: 32 (over z, core).
Axes of the slice: x: 4, y: 4, z: 16, core: 2. Of those that a mesh axis runs over, the one named last changes fastest.
Arguments:
- coarse: bfloat16 [65536, 1536], P(('img', 'tile')), parts along dimension 0, may hold values from -6 to 6
- fine_embed: bfloat16 [262144, 1536], P(('img', 'tile')), parts along dimension 0, may hold values from -6 to 6
- fine_gain: float32 [1536], replicated, may hold values from 0.1 to 1.9
- coarse_gain: float32 [1536], replicated, may hold values from 0.1 to 1.9
- w_query: bfloat16 [1536, 768], P('tile'), may hold values from -120 to 120
- w_kv: bfloat16 [1536, 1536], P('tile'), may hold values from -0.15625 to 0.15625
- w_out: bfloat16 [768, 1536], P('tile'), may hold values from -1.75 to 1.75
- readers: int32 [512, 16], P('img'), parts along dimension 0, may hold values from 0 to 31, all different within a row
- picks: int32 [512, 16], P('img'), parts along dimension 0, may hold values from 0 to 7
Outputs:
- attended: bfloat16 [262144, 1536], P(('img', 'tile')), parts along dimension 0
The draws below stay inside these ranges and needn't reach their ends.
There are 16 independent parts, one for each index of `img`. The reference program is written for one: setup_inputs(seed, part) draws one part's arguments, and reference() takes and returns one part's arrays. A program takes and returns all parts, laid end to end along the dimension named above; an argument that names none is the same for every part. Nothing has to cross between parts.
Inputs may be any that keep to these rules, and one draw needn't show every extreme that they name: `readers`: row t names 16 different strips; every strip is named by some tile.
All inputs are finite; a program needn't handle non-finite values.
Results may differ from the reference program's by a relative error of at most 0.035.
The reference program's roundings to bfloat16 on the way (of `upsampled`, `fine_normed`, `query`, `coarse_normed`, `keyval`, `weights` and `mixed`) count: a program that leaves them out, or rounds other values in their place, can miss the bound.
Values may be sent and summed in bfloat16 or wider, within the bound.
A program may use at most 64 MiB of HBM per device.

```python
import jax
import jax.numpy as jnp
from jax import lax

D = 1536
HEADS = 12
HDIM = 64
CW = 128
SROWS = 1
BLOCK = 16
HD = 768
NSUB = 8
READS = 16
NC = 4096
NF = 16384
FT = 512
N_TILE = 32


def draw_w_query(key, part):
    key = jax.random.fold_in(key, 11)
    base_key = jax.random.fold_in(key, 0)
    values = jax.random.truncated_normal(base_key, -4.0, 4.0, (D, HD), jnp.float32) * D ** (-0.5)
    return values.astype(jnp.bfloat16)


def plant(result, stream_key, smallest, largest):
    spot = [jax.random.randint(jax.random.fold_in(stream_key, axis), (), 0, length) for axis, length in enumerate(result.shape)]
    longest = result.shape.index(max(result.shape))
    next_to = spot[:longest] + [(spot[longest] + 1) % result.shape[longest]] + spot[longest + 1:]
    return result.at[tuple(spot)].set(smallest).at[tuple(next_to)].set(largest)


def levels(own_key, shape, pieces, least, high):
    def one(position, blocks):
        heights = jax.random.uniform(jax.random.fold_in(jax.random.fold_in(own_key, 6), position), (blocks,), jnp.float32, least / len(pieces), high / len(pieces))
        return jnp.repeat(jnp.exp(heights), shape[position] // blocks).reshape((-1,) + (1,) * (len(shape) - position - 1))

    factor_of = one(*pieces[0])
    for cut in pieces[1:]:
        factor_of = factor_of * one(*cut)
    return factor_of


def different_ones(key, rows, count, top, lift):
    order = jax.random.permutation(jax.random.fold_in(key, 1), count)
    favour = order
    for power in range(3):
        favour = favour * favour // count
    favour = favour * lift // count
    tickets = jax.random.randint(jax.random.fold_in(key, 2), (rows, count), 0, 4096) + favour
    fixed_rows = jax.random.permutation(jax.random.fold_in(key, 3), rows)[jnp.arange(count) % rows]
    tickets = jnp.where(jnp.arange(rows)[:, None] == fixed_rows[None, :], 1 << 14, tickets)
    priority = tickets * count + jnp.arange(count)
    return lax.top_k(priority.astype(jnp.int32), top)[1].astype(jnp.int32)


def scatter_about(key, dims, scale, most, pieces=(), dtype=jnp.bfloat16):
    values = jax.random.normal(key, dims, jnp.float32) * scale
    if len(pieces) > 0:
        values = levels(key, dims, pieces, -0.22, 0.18) * values
    return jnp.clip(values, min=-most, max=most).astype(dtype)


def setup_inputs(seed: int = 0, part: int = 0) -> dict:
    key_list = jax.random.split(jax.random.key(seed), 10)
    own_keys = jax.random.split(jax.random.fold_in(key_list[9], part), 10)
    return {
        "coarse": scatter_about(own_keys[0], (NC, D), 1.0, 6.0, ((0, 32),)),
        "fine_embed": scatter_about(own_keys[1], (NF, D), 1.0, 6.0, ((0, 32),)),
        "fine_gain": jnp.clip(1.0 + 0.18 * jax.random.normal(key_list[2], (D,), jnp.float32), 0.1, 1.9),
        "coarse_gain": jnp.clip(1.0 + 0.18 * jax.random.normal(key_list[3], (D,), jnp.float32), 0.1, 1.9),
        "w_query": draw_w_query(jax.random.fold_in(key_list[9], 71), part),
        "w_kv": scatter_about(key_list[5], (D, 2 * HD), D ** -0.5, 0.15625, ((0, 32),)),
        "w_out": scatter_about(key_list[6], (HD, D), HEADS ** -0.5, 1.75, ((0, 32),)),
        "readers": different_ones(own_keys[7], N_TILE, N_TILE, READS, 8192),
        "picks": plant(jax.random.randint(own_keys[8], (N_TILE, READS), 0, NSUB), jax.random.fold_in(own_keys[8], 1), 0, NSUB - 1).astype(jnp.int32),
    }


EPSILON = 1e-06

def normalize(values, gain_vector):
    widened = values.astype(jnp.float32)
    inverse = lax.rsqrt(lax.optimization_barrier(jnp.mean(widened * widened, axis=-1, keepdims=True)) + EPSILON)
    return widened * inverse * gain_vector

def attend(query, keyval):
    row_count = query.shape[0]
    key_count = keyval.shape[0]
    inner = HEADS * HDIM
    query_heads = query.astype(jnp.float32).reshape(row_count, HEADS, HDIM)
    key_heads = keyval[:, :inner].astype(jnp.float32).reshape(key_count, HEADS, HDIM)
    value_heads = keyval[:, inner:].astype(jnp.float32).reshape(key_count, HEADS, HDIM)
    scores = jnp.einsum('qhd,khd->hqk', query_heads, key_heads) * HDIM ** (-0.5)
    maximum = lax.optimization_barrier(jnp.max(scores, axis=-1, keepdims=True))
    exponent = jnp.exp(scores - maximum)
    weights = (exponent / lax.optimization_barrier(jnp.sum(exponent, axis=-1, keepdims=True))).astype(jnp.bfloat16)
    mixed = jnp.einsum('hqk,khd->qhd', weights.astype(jnp.float32), value_heads)
    return mixed.astype(jnp.bfloat16).reshape(row_count, inner)

def reference(coarse, fine_embed, fine_gain, coarse_gain, w_query, w_kv, w_out, readers, picks):
    tile_rows = N_TILE // 8
    block_cols = CW // 8
    coarse_grid = coarse.reshape(tile_rows, 8 * SROWS, 8, block_cols, D).transpose(0, 2, 1, 3, 4)
    upsampled = jnp.repeat(jnp.repeat(coarse_grid, 2, axis=2), 2, axis=3).reshape(NF, D)
    hidden = fine_embed.astype(jnp.float32) + upsampled.astype(jnp.float32)
    fine_normed = normalize(hidden, fine_gain).astype(jnp.bfloat16)
    query = jnp.dot(fine_normed, w_query, preferred_element_type=jnp.float32).astype(jnp.bfloat16)
    coarse_normed = normalize(coarse, coarse_gain).astype(jnp.bfloat16)
    keyval = jnp.dot(coarse_normed, w_kv, preferred_element_type=jnp.float32).astype(jnp.bfloat16)
    keyval_blocks = keyval.reshape(N_TILE, NSUB, BLOCK, 2 * HD)
    tile_queries = query.reshape(N_TILE, FT, HD)

    def per_tile(inputs):
        tile_query, tile_readers, tile_picks = inputs
        chosen = keyval_blocks[tile_readers.astype(jnp.int32), tile_picks.astype(jnp.int32)]
        return attend(tile_query, chosen.reshape(READS * BLOCK, 2 * HD))
    mixed = lax.map(per_tile, (tile_queries, readers, picks)).reshape(NF, HD)
    return jnp.dot(mixed, w_out, preferred_element_type=jnp.float32).astype(jnp.bfloat16)
```

```python
import functools

import jax
import jax.numpy as jnp
from jax import lax
from jax.experimental import pallas as pl
from jax.experimental.pallas import tpu as pltpu
from jax.sharding import PartitionSpec as P

HEADS = 12
HDIM = 64
BLOCK = 16
NZ = 16
NT = 32
D = 1536
HD = 768
LONG = 5
SHORT = 4
EPSILON = 1e-06
MESH = pl.DeviceIdType.MESH


def wrap(value, size):
    return lax.rem(value + size, size)


def gather_kernel(
    coarse_ref, shard_ref, blk_ref, w_ref, x_ref, up_ref,
    l1, l2, l3, l4, l5, s1, s2, s3, s4, stage, far_l, far_s, local_sem, zw_send, zw_recv,
    c_send, c_recv, far_send, far_recv, near_send, near_recv, up_send, up_recv,
    a_send, a_recv, b_send, b_recv, d_send, d_recv,
):
    img, tile = lax.axis_index("img"), lax.axis_index("tile")
    z, core = tile // 2, lax.rem(tile, 2)
    other = 1 - core
    sign = 1 - 2 * core
    gx, gy = img // 4, lax.rem(img, 4)
    a = jnp.where(core == 0, gx, gy)
    b = jnp.where(core == 0, gy, gx)

    def along(steps):
        return wrap(z + sign * steps, NZ)

    def on_z(steps, which):
        return {"img": img, "tile": along(steps) * 2 + which}

    def on_plane(first, second):
        first, second = wrap(first, 4), wrap(second, 4)
        return {"img": jnp.where(core == 0, first * 4 + second, second * 4 + first), "tile": tile}

    sibling = {"img": img, "tile": z * 2 + other}
    a_up, a_down = on_plane(a + 1, b), on_plane(a - 1, b)
    b_up, b_down = on_plane(a, b + 1), on_plane(a, b - 1)
    ahead, behind = on_z(1, core), on_z(-1, core)

    partners = [sibling, a_up, a_down, b_up, b_down]
    partners += [on_z(j, which) for j in (-3, -2, -1, 1, 2, 3) for which in (core, other)]
    barrier = pltpu.get_barrier_semaphore()
    for partner in partners:
        pl.semaphore_signal(barrier, inc=1, device_id=partner, device_id_type=MESH)
    pl.semaphore_wait(barrier, len(partners))

    def remote(src, dst, send, recv, device):
        return pltpu.make_async_remote_copy(
            src_ref=src, dst_ref=dst, send_sem=send, recv_sem=recv, device_id=device, device_id_type=MESH
        )

    pending = []

    def go(copy):
        copy.start()
        pending.append(copy)
        return copy

    bp = lax.rem(b, 2)

    def zw_copy(step, forward):
        source = along(-(step - 1) if forward else step - 1)
        where = w_ref.at[a, bp, :, source, core]
        src = shard_ref.at[a, bp] if step == 1 else where
        slot = step - 1 if forward else 8 + step - 1
        return remote(src, where, zw_send.at[slot], zw_recv.at[slot], ahead if forward else behind)

    long_buf = [coarse_ref, l1, l2, l3, l4, l5]
    short_buf = [coarse_ref, s1, s2, s3, s4]

    def c_copy(step, half, forward):
        bufs = long_buf if forward else short_buf
        slot = 2 * (step - 1 if forward else LONG + step - 1) + half
        part = pl.ds(4 * half, 4)
        return remote(
            bufs[step - 1].at[part], bufs[step].at[part], c_send.at[slot], c_recv.at[slot],
            ahead if forward else behind,
        )

    zw, cc = {}, {}

    def zw_start(step):
        zw[step, True] = go(zw_copy(step, True))
        if step <= 7:
            zw[step, False] = go(zw_copy(step, False))

    def zw_wait(step):
        zw[step, True].wait_recv()
        if step <= 7:
            zw[step, False].wait_recv()

    def c_start(step, half):
        if step <= LONG:
            cc[step, half, True] = go(c_copy(step, half, True))
        if step <= SHORT:
            cc[step, half, False] = go(c_copy(step, half, False))

    def c_wait(step, half):
        if step <= LONG:
            cc[step, half, True].wait_recv()
        if step <= SHORT:
            cc[step, half, False].wait_recv()

    conditional = []

    def share(buf, steps, index, distance):
        strip = along(steps) * 2 + core
        x_ref[core, distance] = buf[blk_ref[tile, strip]]
        stage[index] = buf[blk_ref[z * 2 + other, strip]]
        go(remote(stage.at[index], x_ref.at[core, distance], near_send.at[index], near_recv.at[index], sibling))
        if abs(steps) <= 3:
            position = lax.rem(z, 4) + sign * steps
            inside = (position >= 0) & (position < 4)
            column = lax.rem(tile, 8)
            column_other = lax.rem(z * 2 + other, 8)
            kept = jnp.clip(position, 0, 3)
            row = 2 * kept + core
            sent = remote(
                buf.at[column_other], up_ref.at[row], up_send.at[index], up_recv.at[kept], sibling
            )

            @pl.when(inside)
            def _():
                up_ref[row] = buf[column]
                sent.start()

            conditional.append((inside, sent))

    def share_step(step):
        if step == 0:
            share(coarse_ref, 0, 0, 0)
            return
        if step <= LONG:
            share(long_buf[step], -step, step, step)
        if step <= SHORT:
            share(short_buf[step], step, LONG + step, NZ - step)

    far = []

    def send_far(forward):
        buf = l5 if forward else s4
        held = LONG if forward else SHORT
        picked = far_l if forward else far_s
        strip = along(-LONG if forward else SHORT) * 2 + core
        for j in (3, 2, 1):
            target = along(j if forward else -j)
            distance = held + j if forward else NZ - held - j
            for e in range(2):
                which = core if e == 0 else other
                slot = (0 if forward else 6) + 2 * (j - 1) + e
                picked[2 * (j - 1) + e] = buf[blk_ref[target * 2 + which, strip]]
                far.append(go(remote(
                    picked.at[2 * (j - 1) + e], x_ref.at[core, distance], far_send.at[slot], far_recv.at[slot],
                    {"img": img, "tile": target * 2 + which},
                )))

    own = pltpu.make_async_copy(shard_ref.at[a, bp], w_ref.at[a, bp, :, z, core], local_sem)
    own.start()
    zw_start(1)
    c_start(1, 0)
    c_start(1, 1)
    share_step(0)
    for step in (2, 3, 4):
        zw_wait(step - 1)
        zw_start(step)
    c_wait(1, 0)
    c_start(2, 0)
    zw_wait(4)
    zw_start(5)
    c_wait(1, 1)
    c_start(2, 1)
    share_step(1)
    for step in (6, 7, 8):
        zw_wait(step - 1)
        zw_start(step)
    c_wait(2, 0)
    c_start(3, 0)
    c_wait(2, 1)
    c_start(3, 1)
    zw_wait(8)
    own.wait()

    def piece(position):
        return w_ref.at[wrap(position, 4), bp, :, :, core]

    def half_piece(position, half):
        return w_ref.at[wrap(position, 4), bp, :, pl.ds(8 * half, 8), core]

    a1 = go(remote(piece(a), piece(a), a_send.at[0], a_recv.at[0], a_up))
    a2 = go(remote(piece(a), piece(a), a_send.at[1], a_recv.at[1], a_down))
    share_step(2)
    c_wait(3, 0)
    c_start(4, 0)
    a1.wait_recv()
    a2.wait_recv()
    a3 = go(remote(half_piece(a - 1, 0), half_piece(a - 1, 0), a_send.at[2], a_recv.at[2], a_up))
    a4 = go(remote(half_piece(a + 1, 1), half_piece(a + 1, 1), a_send.at[3], a_recv.at[3], a_down))
    c_wait(3, 1)
    c_start(4, 1)
    share_step(3)
    a3.wait_recv()
    a4.wait_recv()

    b1 = go(remote(
        w_ref.at[:, bp, :, pl.ds(0, 8), core], w_ref.at[:, bp, :, pl.ds(0, 8), core], b_send.at[0], b_recv.at[0], b_up,
    ))
    b2 = go(remote(
        w_ref.at[:, bp, :, pl.ds(8, 8), core], w_ref.at[:, bp, :, pl.ds(8, 8), core], b_send.at[1], b_recv.at[1], b_down,
    ))
    d1 = go(remote(w_ref.at[:, bp, :, :, core], w_ref.at[:, bp, :, :, core], d_send.at[0], d_recv.at[0], sibling))
    c_wait(4, 0)
    c_start(5, 0)
    c_wait(4, 1)
    c_start(5, 1)
    send_far(False)
    share_step(4)
    c_wait(5, 0)
    c_wait(5, 1)
    send_far(True)
    share_step(5)
    b1.wait_recv()
    b2.wait_recv()
    d2 = go(remote(
        w_ref.at[:, 1 - bp, :, :, core], w_ref.at[:, 1 - bp, :, :, core], d_send.at[1], d_recv.at[1], sibling,
    ))
    for copy in far:
        copy.wait_recv()
    for index in range(LONG + SHORT + 1):
        remote(stage.at[index], x_ref.at[core, index], near_send.at[index], near_recv.at[index], sibling).wait_recv()
    for row in range(4):
        remote(coarse_ref.at[0], up_ref.at[row], up_send.at[row], up_recv.at[row], sibling).wait_recv()
    d1.wait_recv()
    d2.wait_recv()
    for copy in pending:
        copy.wait_send()
    for inside, copy in conditional:
        pl.when(inside)(copy.wait_send)


def gather(coarse, shard, blk):
    vmem = pl.BlockSpec(memory_space=pltpu.VMEM)
    strip = pltpu.VMEM((8, BLOCK, D), jnp.bfloat16)
    dma = pltpu.SemaphoreType.DMA
    near = LONG + SHORT + 1
    return pl.pallas_call(
        gather_kernel,
        out_shape=(
            jax.ShapeDtypeStruct((4, 2, 3, NZ, 2, 48, 128), jnp.bfloat16),
            jax.ShapeDtypeStruct((2, NZ, BLOCK, D), jnp.bfloat16),
            jax.ShapeDtypeStruct((8, BLOCK, D), jnp.bfloat16),
        ),
        in_specs=[vmem, vmem, pl.BlockSpec(memory_space=pltpu.SMEM)],
        out_specs=(vmem, vmem, vmem),
        scratch_shapes=[strip] * (LONG + SHORT) + [
            pltpu.VMEM((near, BLOCK, D), jnp.bfloat16),
            pltpu.VMEM((6, BLOCK, D), jnp.bfloat16),
            pltpu.VMEM((6, BLOCK, D), jnp.bfloat16),
            dma,
            dma((16,)), dma((16,)),
            dma((2 * (LONG + SHORT),)), dma((2 * (LONG + SHORT),)),
            dma((12,)), dma((12,)),
            dma((near,)), dma((near,)),
            dma((near,)), dma((4,)),
            dma((4,)), dma((4,)),
            dma((2,)), dma((2,)),
            dma((2,)), dma((2,)),
        ],
        compiler_params=pltpu.CompilerParams(
            collective_id=0, has_side_effects=True, vmem_limit_bytes=56 << 20
        ),
    )(coarse, shard, blk)


def normalized(values, gain):
    inverse = lax.rsqrt(jnp.mean(values * values, axis=-1, keepdims=True) + EPSILON)
    return (values * inverse * gain).astype(jnp.bfloat16)


def compute_kernel(
    slot_ref, fine_ref, up_ref, x_ref, w_ref, fine_gain_ref, coarse_gain_ref, out_ref,
    fine_n, coarse_n, query, keyval, mixed, w_out,
):
    rows = lax.broadcasted_iota(jnp.int32, (32, BLOCK), 0) // 2
    spread = (rows == lax.broadcasted_iota(jnp.int32, (32, BLOCK), 1)).astype(jnp.bfloat16)

    @pl.loop(0, 8)
    def _(i):
        up = jnp.dot(spread, up_ref[i], preferred_element_type=jnp.float32)
        for half in range(2):
            part = pl.ds(pl.multiple_of(i * 64 + half * 32, 32), 32)
            hidden = fine_ref[part, :].astype(jnp.float32) + up
            fine_n[part, :] = normalized(hidden, fine_gain_ref[...])

    @pl.loop(0, 16)
    def _(r):
        slot = slot_ref[r]
        values = x_ref[slot // NZ, lax.rem(slot, NZ)].astype(jnp.float32)
        coarse_n[pl.ds(pl.multiple_of(r * BLOCK, BLOCK), BLOCK), :] = normalized(values, coarse_gain_ref[...])

    def pair(first):
        return jnp.concatenate([w_ref[first].reshape(D, 128), w_ref[first + 1].reshape(D, 128)], axis=1)

    @pl.loop(0, 3)
    def _(j):
        query[:, pl.ds(pl.multiple_of(j * 256, 256), 256)] = jnp.dot(
            fine_n[...], pair(2 * j), preferred_element_type=jnp.float32
        ).astype(jnp.bfloat16)

    @pl.loop(0, 6)
    def _(j):
        keyval[:, pl.ds(pl.multiple_of(j * 256, 256), 256)] = jnp.dot(
            coarse_n[...], pair(6 + 2 * j), preferred_element_type=jnp.float32
        ).astype(jnp.bfloat16)

    @pl.loop(0, NZ)
    def _(k):
        for j in range(6):
            even = w_ref[18 + j, k, 0].astype(jnp.float32)
            odd = w_ref[18 + j, k, 1].astype(jnp.float32)
            part = pl.ds(pl.multiple_of(k * 48, 48), 48)
            for half in range(2):
                lanes = pl.ds((j + 6 * half) * 128, 128)
                cut = slice(24 * half, 24 * half + 24)
                w_out[part, lanes] = jnp.concatenate([even[cut], odd[cut]], axis=0).astype(jnp.bfloat16)

    @pl.loop(0, HEADS // 2)
    def _(p):
        lanes = pl.ds(pl.multiple_of(p * 128, 128), 128)
        value_lanes = pl.ds(pl.multiple_of(HD + p * 128, 128), 128)
        queries, keys, values = query[:, lanes], keyval[:, lanes], keyval[:, value_lanes]
        results = []
        for h in range(2):
            cut = slice(h * HDIM, h * HDIM + HDIM)
            scores = lax.dot_general(
                queries[:, cut], keys[:, cut], (((1,), (1,)), ((), ())), preferred_element_type=jnp.float32
            ) * HDIM ** (-0.5)
            exponent = jnp.exp(scores - jnp.max(scores, axis=-1, keepdims=True))
            weights = (exponent / jnp.sum(exponent, axis=-1, keepdims=True)).astype(jnp.bfloat16)
            results.append(jnp.dot(weights, values[:, cut], preferred_element_type=jnp.float32))
        mixed[:, lanes] = jnp.concatenate(results, axis=1).astype(jnp.bfloat16)

    @pl.loop(0, 6)
    def _(j):
        lanes = pl.ds(pl.multiple_of(j * 256, 256), 256)
        out_ref[:, lanes] = jnp.dot(
            mixed[...], w_out[:, lanes], preferred_element_type=jnp.float32
        ).astype(jnp.bfloat16)


def compute(slots, fine, up, x, w, fine_gain, coarse_gain):
    vmem = pl.BlockSpec(memory_space=pltpu.VMEM)
    return pl.pallas_call(
        compute_kernel,
        out_shape=jax.ShapeDtypeStruct(fine.shape, jnp.bfloat16),
        in_specs=[pl.BlockSpec(memory_space=pltpu.SMEM)] + [vmem] * 6,
        out_specs=vmem,
        scratch_shapes=[
            pltpu.VMEM((512, D), jnp.bfloat16),
            pltpu.VMEM((256, D), jnp.bfloat16),
            pltpu.VMEM((512, HD), jnp.bfloat16),
            pltpu.VMEM((256, D), jnp.bfloat16),
            pltpu.VMEM((512, HD), jnp.bfloat16),
            pltpu.VMEM((HD, D), jnp.bfloat16),
        ],
        compiler_params=pltpu.CompilerParams(vmem_limit_bytes=56 << 20),
    )(slots, fine, up, x, w, fine_gain, coarse_gain)


def body(coarse, fine_embed, fine_gain, coarse_gain, w_query, w_kv, w_out, readers, picks):
    tile = lax.axis_index("tile")
    z = tile // 2
    strips = jnp.arange(NT, dtype=jnp.int32)
    blk = jnp.sum(jnp.where(readers[:, :, None] == strips, picks[:, :, None], 0), axis=1)
    mine = lax.dynamic_index_in_dim(readers, tile, 0, keepdims=False)
    lane = mine % 2
    slots = lane * NZ + ((z - mine // 2) * (1 - 2 * lane)) % NZ

    def slabs(w):
        return w.reshape(48, -1, 128).transpose(1, 0, 2)

    out_pairs = w_out.reshape(24, 2, 6, 128).transpose(2, 1, 0, 3).reshape(6, 48, 128)
    shard = jnp.concatenate([slabs(w_query), slabs(w_kv), out_pairs], axis=0).reshape(4, 2, 3, 48, 128)
    w, x, up = gather(coarse.reshape(8, BLOCK, D), shard, blk)
    return compute(
        slots, fine_embed, up, x, w.reshape(24, NZ, 2, 48, 128), fine_gain.reshape(1, D), coarse_gain.reshape(1, D)
    )


def solution(mesh):
    placed = (
        P(("img", "tile"), None),
        P(("img", "tile"), None),
        P(),
        P(),
        P("tile", None),
        P("tile", None),
        P("tile", None),
        P("img", None),
        P("img", None),
    )
    return jax.shard_map(
        body, mesh=mesh, in_specs=placed, out_specs=P(("img", "tile"), None), check_vma=False
    )
```

```python
import jax
import jax.numpy as jnp
from jax import lax
from jax.experimental import pallas as pl
from jax.experimental.pallas import tpu as pltpu
from jax.sharding import PartitionSpec as P

HEADS = 12
HDIM = 64
BLOCK = 16
NZ = 16
NT = 32
D = 1536
HD = 768
LONG = 5
SHORT = 4
EPSILON = 1e-06
LOG2E = 1.4426950408889634
MESH = pl.DeviceIdType.MESH


def wrap(value, size):
    return lax.rem(value + size, size)


def normalized(values, gain):
    inverse = lax.rsqrt(jnp.mean(values * values, axis=-1, keepdims=True) + EPSILON)
    return (values * inverse * gain).astype(jnp.bfloat16)


def kernel(
    coarse_ref, wq_ref, wkv_ref, wo_ref, blk_ref, readers_ref, fine_hbm, fine_gain_ref, coarse_gain_ref, out_hbm,
    w_ref, x_ref, up_ref, l1, l2, l3, l4, l5, s1, s2, s3, s4, stage, far_l, far_s,
    fine, fine_n, coarse_n, query, keyval, mixed, w_out, out, gains,
    local_sem, out_sem, zw_send, zw_recv, c_send, c_recv, far_send, far_recv, near_send, near_recv, up_send, up_recv,
    a_send, a_recv, b_send, b_recv, d_send, d_recv,
):
    img, tile = lax.axis_index("img"), lax.axis_index("tile")
    z, core = tile // 2, lax.rem(tile, 2)
    other = 1 - core
    sign = 1 - 2 * core
    gx, gy = img // 4, lax.rem(img, 4)
    a = jnp.where(core == 0, gx, gy)
    b = jnp.where(core == 0, gy, gx)
    bp = lax.rem(b, 2)

    fine_copy = pltpu.make_async_copy(fine_hbm, fine, local_sem)
    fine_copy.start()

    def along(steps):
        return wrap(z + sign * steps, NZ)

    def on_z(steps, which):
        return {"img": img, "tile": along(steps) * 2 + which}

    def on_plane(first, second):
        first, second = wrap(first, 4), wrap(second, 4)
        return {"img": jnp.where(core == 0, first * 4 + second, second * 4 + first), "tile": tile}

    sibling = {"img": img, "tile": z * 2 + other}
    a_up, a_down = on_plane(a + 1, b), on_plane(a - 1, b)
    b_up, b_down = on_plane(a, b + 1), on_plane(a, b - 1)
    ahead, behind = on_z(1, core), on_z(-1, core)

    partners = [sibling, a_up, a_down, b_up, b_down]
    partners += [on_z(j, which) for j in (-3, -2, -1, 1, 2, 3) for which in (core, other)]
    barrier = pltpu.get_barrier_semaphore()
    for partner in partners:
        pl.semaphore_signal(barrier, inc=1, device_id=partner, device_id_type=MESH)

    piece_index = 2 * a + bp

    @pl.when(piece_index < 2)
    def _():
        for i in range(3):
            lanes = pl.ds(pl.multiple_of((3 * piece_index + i) * 128, 128), 128)
            w_ref[a, bp, i, z, core] = wq_ref[:, lanes]

    @pl.when((piece_index >= 2) & (piece_index < 6))
    def _():
        for i in range(3):
            lanes = pl.ds(pl.multiple_of((3 * piece_index + i - 6) * 128, 128), 128)
            w_ref[a, bp, i, z, core] = wkv_ref[:, lanes]

    @pl.when(piece_index >= 6)
    def _():
        for i in range(3):
            slab = 3 * piece_index + i - 18
            upper = wo_ref[:, pl.ds(pl.multiple_of(slab * 128, 128), 128)].astype(jnp.float32)
            lower = wo_ref[:, pl.ds(pl.multiple_of((slab + 6) * 128, 128), 128)].astype(jnp.float32)
            w_ref[a, bp, i, z, core] = jnp.concatenate([upper, lower], axis=0).astype(jnp.bfloat16)

    pl.semaphore_wait(barrier, len(partners))

    def remote(src, dst, send, recv, device):
        return pltpu.make_async_remote_copy(
            src_ref=src, dst_ref=dst, send_sem=send, recv_sem=recv, device_id=device, device_id_type=MESH
        )

    pending = []

    def go(copy):
        copy.start()
        pending.append(copy)
        return copy

    def drain():
        for copy in pending:
            copy.wait_send()
        pending.clear()

    def place(m):
        return along(-m if m <= 8 else m - 8)

    def group(step):
        return [0] if step == 0 else [8] if step == 8 else [step, 8 + step]

    zw, x1, x2, y, d1, d2, cc = {}, {}, {}, {}, {}, {}, {}

    def zw_start(step):
        for m in group(step):
            where = w_ref.at[a, bp, :, along(1 - m if m <= 8 else m - 9), core]
            zw[m] = go(remote(where, where, zw_send.at[m], zw_recv.at[m], ahead if m <= 8 else behind))

    def x1_start(step):
        for m in group(step):
            where = w_ref.at[a, bp, :, place(m), core]
            for k, device in enumerate((a_up, a_down)):
                slot = 2 * m + k
                x1[m, k] = go(remote(where, where, a_send.at[slot], a_recv.at[slot], device))

    def x2_start(step):
        for m in group(step):
            rising = m < 8
            where = w_ref.at[wrap(a - 1 if rising else a + 1, 4), bp, :, place(m), core]
            x2[m] = go(remote(where, where, a_send.at[32 + m], a_recv.at[32 + m], a_up if rising else a_down))

    def y_start(step):
        for m in group(step):
            where = w_ref.at[:, bp, :, place(m), core]
            y[m] = go(remote(where, where, b_send.at[m], b_recv.at[m], b_up if m < 8 else b_down))
            d1[m] = go(remote(where, where, d_send.at[m], d_recv.at[m], sibling))

    def d2_start(step):
        for m in group(step):
            where = w_ref.at[:, 1 - bp, :, place(m), core]
            d2[m] = go(remote(where, where, d_send.at[16 + m], d_recv.at[16 + m], sibling))

    long_buf = [coarse_ref, l1, l2, l3, l4, l5]
    short_buf = [coarse_ref, s1, s2, s3, s4]

    def c_copy(step, half, forward):
        bufs = long_buf if forward else short_buf
        slot = 2 * (step - 1 if forward else LONG + step - 1) + half
        part = pl.ds(4 * half, 4)
        return remote(
            bufs[step - 1].at[part], bufs[step].at[part], c_send.at[slot], c_recv.at[slot],
            ahead if forward else behind,
        )

    def c_start(step, half):
        if step <= LONG:
            cc[step, half, True] = go(c_copy(step, half, True))
        if step <= SHORT:
            cc[step, half, False] = go(c_copy(step, half, False))

    def c_pass(step, half):
        if step <= LONG:
            cc[step, half, True].wait_recv()
        if step <= SHORT:
            cc[step, half, False].wait_recv()
        if step < LONG:
            c_start(step + 1, half)

    conditional = []

    def share(buf, steps, index, distance):
        strip = along(steps) * 2 + core
        x_ref[core, distance] = buf[blk_ref[tile, strip]]
        stage[index] = buf[blk_ref[z * 2 + other, strip]]
        go(remote(stage.at[index], x_ref.at[core, distance], near_send.at[index], near_recv.at[index], sibling))
        if abs(steps) <= 3:
            position = lax.rem(z, 4) + sign * steps
            inside = (position >= 0) & (position < 4)
            column = lax.rem(tile, 8)
            column_other = lax.rem(z * 2 + other, 8)
            kept = jnp.clip(position, 0, 3)
            row = 2 * kept + core
            sent = remote(
                buf.at[column_other], up_ref.at[row], up_send.at[index], up_recv.at[kept], sibling
            )

            @pl.when(inside)
            def _():
                up_ref[row] = buf[column]
                sent.start()

            conditional.append((inside, sent))

    def share_step(step):
        if step == 0:
            share(coarse_ref, 0, 0, 0)
            return
        if step <= LONG:
            share(long_buf[step], -step, step, step)
        if step <= SHORT:
            share(short_buf[step], step, LONG + step, NZ - step)

    far = []

    def send_far(forward):
        buf = l5 if forward else s4
        held = LONG if forward else SHORT
        picked = far_l if forward else far_s
        strip = along(-LONG if forward else SHORT) * 2 + core
        for j in (3, 2, 1):
            target = along(j if forward else -j)
            distance = held + j if forward else NZ - held - j
            for e in range(2):
                which = core if e == 0 else other
                slot = (0 if forward else 6) + 2 * (j - 1) + e
                picked[2 * (j - 1) + e] = buf[blk_ref[target * 2 + which, strip]]
                far.append(go(remote(
                    picked.at[2 * (j - 1) + e], x_ref.at[core, distance], far_send.at[slot], far_recv.at[slot],
                    {"img": img, "tile": target * 2 + which},
                )))

    def tick(i):
        if i <= 8:
            if i > 0:
                for m in group(i):
                    zw[m].wait_recv()
            if i < 8:
                zw_start(i + 1)
            x1_start(i)
        if 1 <= i <= 9:
            for m in group(i - 1):
                x1[m, 0].wait_recv()
                x1[m, 1].wait_recv()
            x2_start(i - 1)
        if 2 <= i <= 10:
            for m in group(i - 2):
                x2[m].wait_recv()
            y_start(i - 2)
        if i >= 3:
            for m in group(i - 3):
                y[m].wait_recv()
            d2_start(i - 3)

    c_start(1, 0)
    tick(0)
    c_start(1, 1)
    share_step(0)
    tick(1)
    c_pass(1, 0)
    tick(2)
    tick(3)
    c_pass(1, 1)
    tick(4)
    c_pass(2, 0)
    share_step(1)
    tick(5)
    tick(6)
    c_pass(2, 1)
    tick(7)
    c_pass(3, 0)
    share_step(2)
    tick(8)
    tick(9)
    c_pass(3, 1)
    tick(10)
    tick(11)
    share_step(3)
    c_pass(4, 0)

    for index, gain_ref in enumerate((fine_gain_ref, coarse_gain_ref)):
        gains[index] = gain_ref[...].reshape(1, D)
    fine_copy.wait()
    for row in range(4):
        remote(coarse_ref.at[0], up_ref.at[row], up_send.at[row], up_recv.at[row], sibling).wait_recv()

    rows = lax.broadcasted_iota(jnp.int32, (32, BLOCK), 0) // 2
    spread = (rows == lax.broadcasted_iota(jnp.int32, (32, BLOCK), 1)).astype(jnp.bfloat16)

    def fine_norm(first, last):
        @pl.loop(first, last)
        def _(i):
            up = jnp.dot(spread, up_ref[i], preferred_element_type=jnp.float32)
            for half in range(2):
                part = pl.ds(pl.multiple_of(i * 64 + half * 32, 32), 32)
                hidden = fine[part, :].astype(jnp.float32) + up
                fine_n[part, :] = normalized(hidden, gains[0])

    def slab(index):
        return w_ref[index // 6, lax.rem(index // 3, 2), lax.rem(index, 3)].reshape(D, 128)

    def project_query():
        @pl.loop(0, 3)
        def _(j):
            pair = jnp.concatenate([slab(2 * j), slab(2 * j + 1)], axis=1)
            query[:, pl.ds(pl.multiple_of(j * 256, 256), 256)] = jnp.dot(
                fine_n[...], pair, preferred_element_type=jnp.float32
            ).astype(jnp.bfloat16)

    def order_out():
        @pl.loop(0, NZ)
        def _(k):
            part = pl.ds(pl.multiple_of(k * 48, 48), 48)
            for j in range(6):
                even = w_ref[3, j // 3, j % 3, k, 0].astype(jnp.float32)
                odd = w_ref[3, j // 3, j % 3, k, 1].astype(jnp.float32)
                for half in range(2):
                    cut = slice(24 * half, 24 * half + 24)
                    w_out[part, pl.ds((j + 6 * half) * 128, 128)] = jnp.concatenate(
                        [even[cut], odd[cut]], axis=0
                    ).astype(jnp.bfloat16)

    fine_norm(0, 8)
    c_pass(4, 1)
    send_far(False)
    share_step(4)
    c_pass(5, 0)
    for m in range(16):
        d1[m].wait_recv()
        d2[m].wait_recv()
    project_query()
    c_pass(5, 1)
    send_far(True)
    share_step(5)
    order_out()
    drain()
    for inside, copy in conditional:
        pl.when(inside)(copy.wait_send)
    for index in range(LONG + SHORT + 1):
        remote(stage.at[index], x_ref.at[core, index], near_send.at[index], near_recv.at[index], sibling).wait_recv()
    for copy in far:
        copy.wait_recv()

    @pl.loop(0, 16)
    def _(r):
        reader = readers_ref[r, tile]
        lane = lax.rem(reader, 2)
        distance = lax.rem((z - reader // 2) * (1 - 2 * lane) + NZ, NZ)
        values = x_ref[lane, distance].astype(jnp.float32)
        coarse_n[pl.ds(pl.multiple_of(r * BLOCK, BLOCK), BLOCK), :] = normalized(values, gains[1])

    def projected(p):
        pair = jnp.concatenate([slab(6 + p), slab(12 + p)], axis=1)
        return jnp.dot(coarse_n[...], pair, preferred_element_type=jnp.float32).astype(jnp.bfloat16)

    low = lax.broadcasted_iota(jnp.int32, (1, 128), 1) < HDIM
    keyval[0] = projected(0)

    @pl.loop(0, HEADS // 2, unroll=2)
    def _(p):
        lanes = pl.ds(pl.multiple_of(p * 128, 128), 128)
        both = keyval[lax.rem(p, 2)]
        keyval[lax.rem(p + 1, 2)] = projected(jnp.minimum(p + 1, HEADS // 2 - 1))
        keys, values = both[:, :128], both[:, 128:]
        zero, one = jnp.zeros_like(keys), jnp.ones_like(values)
        key_pair = [jnp.where(low, keys, zero), jnp.where(low, zero, keys)]
        value_pair = [jnp.where(low, values, one), jnp.where(low, one, values)]
        queries = query[:, lanes]
        results = []
        for h in range(2):
            scores = lax.dot_general(
                queries, key_pair[h], (((1,), (1,)), ((), ())), preferred_element_type=jnp.float32
            )
            top = jnp.max(scores, axis=-1, keepdims=True)
            exponent = jnp.exp2((scores - top) * (HDIM ** (-0.5) * LOG2E)).astype(jnp.bfloat16)
            results.append(jnp.dot(exponent, value_pair[h], preferred_element_type=jnp.float32))
        total = pltpu.roll(jnp.where(low, results[1], results[0]), HDIM, 1)
        mixed[:, lanes] = (jnp.where(low, results[0], results[1]) / total).astype(jnp.bfloat16)

    for j in range(3):
        lanes = pl.ds(j * 512, 512)
        out[j] = jnp.dot(mixed[...], w_out[:, lanes], preferred_element_type=jnp.float32).astype(jnp.bfloat16)
        pltpu.make_async_copy(out.at[j], out_hbm.at[:, lanes], out_sem.at[j]).start()
    for j in range(3):
        pltpu.make_async_copy(out.at[j], out_hbm.at[:, pl.ds(j * 512, 512)], out_sem.at[j]).wait()


def body(coarse, fine_embed, fine_gain, coarse_gain, w_query, w_kv, w_out, readers, picks):
    strips = jnp.arange(NT, dtype=jnp.int32)
    readers, picks = readers.T, picks.T
    blk = jnp.sum(jnp.where(readers[:, :, None] == strips, picks[:, :, None], 0), axis=0)
    vmem, smem = pl.BlockSpec(memory_space=pltpu.VMEM), pl.BlockSpec(memory_space=pltpu.SMEM)
    hbm = pl.BlockSpec(memory_space=pl.ANY)
    bf16 = jnp.bfloat16
    strip = pltpu.VMEM((8, BLOCK, D), bf16)
    near = LONG + SHORT + 1

    def dma(count):
        return pltpu.SemaphoreType.DMA((count,))

    return pl.pallas_call(
        kernel,
        out_shape=jax.ShapeDtypeStruct(fine_embed.shape, bf16),
        in_specs=[vmem] * 4 + [smem] * 2 + [hbm, vmem, vmem],
        out_specs=hbm,
        scratch_shapes=[
            pltpu.VMEM((4, 2, 3, NZ, 2, 48, 128), bf16),
            pltpu.VMEM((2, NZ, BLOCK, D), bf16),
            strip,
        ] + [strip] * (LONG + SHORT) + [
            pltpu.VMEM((near, BLOCK, D), bf16),
            pltpu.VMEM((6, BLOCK, D), bf16),
            pltpu.VMEM((6, BLOCK, D), bf16),
            pltpu.VMEM((512, D), bf16),
            pltpu.VMEM((512, D), bf16),
            pltpu.VMEM((256, D), bf16),
            pltpu.VMEM((512, HD), bf16),
            pltpu.VMEM((2, 256, 256), bf16),
            pltpu.VMEM((512, HD), bf16),
            pltpu.VMEM((HD, D), bf16),
            pltpu.VMEM((3, 512, 512), bf16),
            pltpu.VMEM((2, 1, D), jnp.float32),
            pltpu.SemaphoreType.DMA, dma(3),
            dma(16), dma(16),
            dma(2 * (LONG + SHORT)), dma(2 * (LONG + SHORT)),
            dma(12), dma(12),
            dma(near), dma(near),
            dma(near), dma(4),
            dma(48), dma(48),
            dma(16), dma(16),
            dma(32), dma(32),
        ],
        compiler_params=pltpu.CompilerParams(
            collective_id=0, has_side_effects=True, vmem_limit_bytes=56 << 20
        ),
    )(coarse.reshape(8, BLOCK, D), w_query, w_kv, w_out, blk, readers, fine_embed, fine_gain, coarse_gain)


def solution(mesh):
    placed = (
        P(("img", "tile"), None),
        P(("img", "tile"), None),
        P(),
        P(),
        P("tile", None),
        P("tile", None),
        P("tile", None),
        P("img", None),
        P("img", None),
    )
    return jax.shard_map(
        body, mesh=mesh, in_specs=placed, out_specs=P(("img", "tile"), None), check_vma=False
    )
```

```python
import jax
import jax.numpy as jnp
from jax import lax
from jax.experimental import pallas as pl
from jax.experimental.pallas import tpu as pltpu
from jax.sharding import PartitionSpec as P

HEADS = 12
HDIM = 64
BLOCK = 16
NZ = 16
NT = 32
D = 1536
HD = 768
LONG = 5
SHORT = 4
EPSILON = 1e-06
LOG2E = 1.4426950408889634
MESH = pl.DeviceIdType.MESH


def wrap(value, size):
    return lax.rem(value + size, size)


def normalized(values, gain):
    inverse = lax.rsqrt(jnp.mean(values * values, axis=-1, keepdims=True) + EPSILON)
    return (values * inverse * gain).astype(jnp.bfloat16)


def kernel(
    coarse_ref, wq_ref, wkv_ref, wo_ref, readers_ref, reader_rows, pick_rows, fine_hbm, fine_gain_ref, coarse_gain_ref, mixed_hbm, w_out_hbm,
    w_ref, x_ref, up_ref, l1, l2, l3, l4, l5, s1, s2, s3, s4, stage, far_l, far_s,
    fine, fine_n, coarse_n, query, keyval, mixed, w_out, gains, blk_rows, blk,
    local_sem, blk_sem, out_sem, zw_send, zw_recv, c_send, c_recv, far_send, far_recv, near_send, near_recv, up_send, up_recv,
    a_send, a_recv, a2_send, a2_recv, b_send, b_recv, d_send, d_recv,
):
    img, tile = lax.axis_index("img"), lax.axis_index("tile")
    z, core = tile // 2, lax.rem(tile, 2)
    other = 1 - core
    sign = 1 - 2 * core
    gx, gy = img // 4, lax.rem(img, 4)
    a = jnp.where(core == 0, gx, gy)
    b = jnp.where(core == 0, gy, gx)
    bp = lax.rem(b, 2)

    fine_copy = pltpu.make_async_copy(fine_hbm, fine, local_sem)
    fine_copy.start()

    def along(steps):
        return wrap(z + sign * steps, NZ)

    def on_z(steps, which):
        return {"img": img, "tile": along(steps) * 2 + which}

    def on_plane(first, second):
        first, second = wrap(first, 4), wrap(second, 4)
        return {"img": jnp.where(core == 0, first * 4 + second, second * 4 + first), "tile": tile}

    sibling = {"img": img, "tile": z * 2 + other}
    a_up, a_down = on_plane(a + 1, b), on_plane(a - 1, b)
    b_up, b_down = on_plane(a, b + 1), on_plane(a, b - 1)
    ahead, behind = on_z(1, core), on_z(-1, core)

    partners = [sibling, a_up, a_down, b_up, b_down]
    partners += [on_z(j, which) for j in (-3, -2, -1, 1, 2, 3) for which in (core, other)]
    barrier = pltpu.get_barrier_semaphore()
    for partner in partners:
        pl.semaphore_signal(barrier, inc=1, device_id=partner, device_id_type=MESH)

    for strip in range(NT):
        blk_rows[strip : strip + 1, :] = jnp.sum(
            jnp.where(reader_rows[...] == strip, pick_rows[...], 0), axis=0, keepdims=True
        )
    blk_copy = pltpu.make_async_copy(blk_rows, blk, blk_sem)
    blk_copy.start()

    piece_index = 2 * a + bp

    @pl.when(piece_index < 2)
    def _():
        for i in range(3):
            lanes = pl.ds(pl.multiple_of((3 * piece_index + i) * 128, 128), 128)
            w_ref[a, bp, i, z, core] = wq_ref[:, lanes]

    @pl.when((piece_index >= 2) & (piece_index < 6))
    def _():
        for i in range(3):
            lanes = pl.ds(pl.multiple_of((3 * piece_index + i - 6) * 128, 128), 128)
            w_ref[a, bp, i, z, core] = wkv_ref[:, lanes]

    @pl.when(piece_index >= 6)
    def _():
        for i in range(3):
            slab = 3 * piece_index + i - 18
            upper = wo_ref[:, pl.ds(pl.multiple_of(slab * 128, 128), 128)].astype(jnp.float32)
            lower = wo_ref[:, pl.ds(pl.multiple_of((slab + 6) * 128, 128), 128)].astype(jnp.float32)
            w_ref[a, bp, i, z, core] = jnp.concatenate([upper, lower], axis=0).astype(jnp.bfloat16)

    pl.semaphore_wait(barrier, len(partners))

    def remote(src, dst, send, recv, device):
        return pltpu.make_async_remote_copy(
            src_ref=src, dst_ref=dst, send_sem=send, recv_sem=recv, device_id=device, device_id_type=MESH
        )

    def go(copy):
        copy.start()

    def drain():
        whole(shards(15), zw_send, zw_recv.at[0]).wait_send()
        whole(w_ref.at[a, bp], a_send, a_recv.at[0]).wait_send()
        whole(shards(16), a2_send, a2_recv.at[0]).wait_send()
        whole(w_ref.at[:, bp, :, :, core], b_send, b_recv.at[0]).wait_send()
        whole(w_ref.at[:, :, :, :, core], d_send, d_recv).wait_send()
        whole(w_ref.at[pl.ds(0, 3), :, :, :, core], c_send, c_recv.at[0]).wait_send()
        whole(x_ref.at[0, pl.ds(0, LONG + SHORT + 1)], near_send, near_recv).wait_send()
        whole(x_ref.at[0, pl.ds(0, 12)], far_send, far_recv).wait_send()
        whole(up_ref.at[pl.ds(0, 4)], up_send, up_recv).wait_send()

    def place(m):
        return along(-m if m <= 8 else m - 8)

    def group(step):
        return [0] if step == 0 else [8] if step == 8 else [step, 8 + step]

    def whole(ref, send, recv):
        return remote(ref, ref, send, recv, sibling)

    def shards(count):
        return w_ref.at[a, bp, :, pl.ds(0, count), core]


    def zw_start(step):
        for m in group(step):
            where = w_ref.at[a, bp, :, along(1 - m if m <= 8 else m - 9), core]
            go(remote(where, where, zw_send, zw_recv.at[step - 1], ahead if m <= 8 else behind))

    def x1_start(step):
        for m in group(step):
            where = w_ref.at[a, bp, :, place(m), core]
            for device in (a_up, a_down):
                go(remote(where, where, a_send, a_recv.at[step], device))

    def x2_start(step):
        for m in group(step):
            rising = m < 8
            where = w_ref.at[wrap(a - 1 if rising else a + 1, 4), bp, :, place(m), core]
            go(remote(where, where, a2_send, a2_recv.at[step], a_up if rising else a_down))

    def y_start(step):
        for m in group(step):
            where = w_ref.at[:, bp, :, place(m), core]
            go(remote(where, where, b_send, b_recv.at[step], b_up if m < 8 else b_down))
            go(remote(where, where, d_send, d_recv, sibling))

    def d2_start(step):
        for m in group(step):
            where = w_ref.at[:, 1 - bp, :, place(m), core]
            go(remote(where, where, d_send, d_recv, sibling))

    long_buf = [coarse_ref, l1, l2, l3, l4, l5]
    short_buf = [coarse_ref, s1, s2, s3, s4]

    def c_copy(step, half, forward):
        bufs = long_buf if forward else short_buf
        slot = 2 * (step - 1) + half
        part = pl.ds(4 * half, 4)
        return remote(
            bufs[step - 1].at[part], bufs[step].at[part], c_send, c_recv.at[slot],
            ahead if forward else behind,
        )

    def c_start(step, half):
        if step <= LONG:
            c_copy(step, half, True).start()
        if step <= SHORT:
            c_copy(step, half, False).start()

    def c_pass(step, half):
        blocks = 8 if step <= SHORT else 4
        whole(x_ref.at[0, pl.ds(0, blocks)], c_send, c_recv.at[2 * (step - 1) + half]).wait_recv()
        if step < LONG:
            c_start(step + 1, half)

    def share(buf, steps, index, distance):
        strip = along(steps) * 2 + core
        x_ref[core, distance] = buf[blk[strip, tile]]
        stage[index] = buf[blk[strip, z * 2 + other]]
        go(remote(stage.at[index], x_ref.at[core, distance], near_send, near_recv, sibling))
        if abs(steps) <= 3:
            position = lax.rem(z, 4) + sign * steps
            inside = (position >= 0) & (position < 4)
            column = lax.rem(tile, 8)
            column_other = lax.rem(z * 2 + other, 8)
            kept = jnp.clip(position, 0, 3)
            row = 2 * kept + core
            sent = remote(
                buf.at[column_other], up_ref.at[row], up_send, up_recv, sibling
            )

            @pl.when(inside)
            def _():
                up_ref[row] = buf[column]
                sent.start()


    def share_step(step):
        if step == 0:
            share(coarse_ref, 0, 0, 0)
            return
        if step <= LONG:
            share(long_buf[step], -step, step, step)
        if step <= SHORT:
            share(short_buf[step], step, LONG + step, NZ - step)

    def send_far(forward):
        buf = l5 if forward else s4
        held = LONG if forward else SHORT
        picked = far_l if forward else far_s
        strip = along(-LONG if forward else SHORT) * 2 + core
        for j in (3, 2, 1):
            target = along(j if forward else -j)
            distance = held + j if forward else NZ - held - j
            for e in range(2):
                which = core if e == 0 else other
                picked[2 * (j - 1) + e] = buf[blk[strip, target * 2 + which]]
                go(remote(
                    picked.at[2 * (j - 1) + e], x_ref.at[core, distance], far_send, far_recv,
                    {"img": img, "tile": target * 2 + which},
                ))

    def tick(i):
        if i <= 8:
            if i > 0:
                whole(shards(len(group(i))), zw_send, zw_recv.at[i - 1]).wait_recv()
            if i < 8:
                zw_start(i + 1)
            x1_start(i)
        if 1 <= i <= 9:
            whole(shards(2 * len(group(i - 1))), a_send, a_recv.at[i - 1]).wait_recv()
            x2_start(i - 1)
        if 2 <= i <= 10:
            whole(shards(len(group(i - 2))), a2_send, a2_recv.at[i - 2]).wait_recv()
            y_start(i - 2)
        if 4 <= i <= 4 + 8:
            count = len(group(i - 4))
            whole(w_ref.at[:, bp, :, pl.ds(0, count), core], b_send, b_recv.at[i - 4]).wait_recv()
            d2_start(i - 4)

    c_start(1, 0)
    tick(0)
    c_start(1, 1)
    blk_copy.wait()
    tick(1)
    c_pass(1, 0)
    share_step(0)
    tick(2)
    c_pass(1, 1)
    share_step(1)
    tick(3)
    c_pass(2, 0)
    tick(4)
    c_pass(2, 1)
    share_step(2)
    tick(5)
    c_pass(3, 0)
    tick(6)
    c_pass(3, 1)
    share_step(3)
    tick(7)
    c_pass(4, 0)
    tick(8)

    for index, gain_ref in enumerate((fine_gain_ref, coarse_gain_ref)):
        gains[index] = gain_ref[...].reshape(1, D)
    fine_copy.wait()
    whole(up_ref.at[pl.ds(0, 4)], up_send, up_recv).wait_recv()

    rows = lax.broadcasted_iota(jnp.int32, (32, BLOCK), 0) // 2
    spread = (rows == lax.broadcasted_iota(jnp.int32, (32, BLOCK), 1)).astype(jnp.bfloat16)

    def fine_norm(first, last):
        @pl.loop(first, last)
        def _(i):
            up = jnp.dot(spread, up_ref[i], preferred_element_type=jnp.float32)
            for half in range(2):
                part = pl.ds(pl.multiple_of(i * 64 + half * 32, 32), 32)
                hidden = fine[part, :].astype(jnp.float32) + up
                fine_n[part, :] = normalized(hidden, gains[0])

    def slab(index):
        return w_ref[index // 6, lax.rem(index // 3, 2), lax.rem(index, 3)].reshape(D, 128)

    def project_query():
        @pl.loop(0, 3)
        def _(j):
            pair = jnp.concatenate([slab(2 * j), slab(2 * j + 1)], axis=1)
            query[:, pl.ds(pl.multiple_of(j * 256, 256), 256)] = jnp.dot(
                fine_n[...], pair, preferred_element_type=jnp.float32
            ).astype(jnp.bfloat16)

    def order_out():
        @pl.loop(0, NZ)
        def _(k):
            part = pl.ds(pl.multiple_of(k * 48, 48), 48)
            for j in range(6):
                even = w_ref[3, j // 3, j % 3, k, 0].astype(jnp.float32)
                odd = w_ref[3, j // 3, j % 3, k, 1].astype(jnp.float32)
                for half in range(2):
                    cut = slice(24 * half, 24 * half + 24)
                    w_out[part, pl.ds((j + 6 * half) * 128, 128)] = jnp.concatenate(
                        [even[cut], odd[cut]], axis=0
                    ).astype(jnp.bfloat16)

    c_pass(4, 1)
    send_far(False)
    share_step(4)
    tick(9)
    fine_norm(0, 4)
    tick(10)
    fine_norm(4, 8)
    tick(11)
    c_pass(5, 0)
    c_pass(5, 1)
    send_far(True)
    share_step(5)
    tick(12)
    whole(w_ref.at[:, :, :, :, core], d_send, d_recv).wait_recv()
    project_query()
    order_out()
    w_out_copy = pltpu.make_async_copy(w_out, w_out_hbm, out_sem.at[HEADS // 2])
    w_out_copy.start()
    drain()
    whole(x_ref.at[0, pl.ds(0, LONG + SHORT + 1)], near_send, near_recv).wait_recv()
    whole(x_ref.at[0, pl.ds(0, 12)], far_send, far_recv).wait_recv()

    @pl.loop(0, 16, unroll=4)
    def _(r):
        reader = readers_ref[r, tile]
        lane = lax.rem(reader, 2)
        distance = lax.rem((z - reader // 2) * (1 - 2 * lane) + NZ, NZ)
        values = x_ref[lane, distance].astype(jnp.float32)
        coarse_n[pl.ds(pl.multiple_of(r * BLOCK, BLOCK), BLOCK), :] = normalized(values, gains[1])

    def projected(p):
        pair = jnp.concatenate([slab(6 + p), slab(12 + p)], axis=1)
        return jnp.dot(coarse_n[...], pair, preferred_element_type=jnp.float32).astype(jnp.bfloat16)

    def mixed_copy(p):
        lanes = pl.ds(pl.multiple_of(p * 128, 128), 128)
        return pltpu.make_async_copy(mixed.at[p], mixed_hbm.at[:, lanes], out_sem.at[p])

    low = lax.broadcasted_iota(jnp.int32, (1, 128), 1) < HDIM
    keyval[0] = projected(0)

    @pl.loop(0, HEADS // 2, unroll=2)
    def _(p):
        lanes = pl.ds(pl.multiple_of(p * 128, 128), 128)
        both = keyval[lax.rem(p, 2)]
        keyval[lax.rem(p + 1, 2)] = projected(jnp.minimum(p + 1, HEADS // 2 - 1))
        keys, values = both[:, :128], both[:, 128:]
        zero, one = jnp.zeros_like(keys), jnp.ones_like(values)
        key_pair = [jnp.where(low, keys, zero), jnp.where(low, zero, keys)]
        value_pair = [jnp.where(low, values, one), jnp.where(low, one, values)]
        queries = query[:, lanes]
        results = []
        for h in range(2):
            scores = lax.dot_general(
                queries, key_pair[h], (((1,), (1,)), ((), ())), preferred_element_type=jnp.float32
            )
            top = jnp.max(scores, axis=-1, keepdims=True)
            exponent = jnp.exp2((scores - top) * (HDIM ** (-0.5) * LOG2E)).astype(jnp.bfloat16)
            results.append(jnp.dot(exponent, value_pair[h], preferred_element_type=jnp.float32))
        total = pltpu.roll(jnp.where(low, results[1], results[0]), HDIM, 1)
        mixed[p] = (jnp.where(low, results[0], results[1]) / total).astype(jnp.bfloat16)
        mixed_copy(p).start()

    for p in range(HEADS // 2):
        mixed_copy(p).wait()
    w_out_copy.wait()


def body(coarse, fine_embed, fine_gain, coarse_gain, w_query, w_kv, w_out, readers, picks):
    vmem, smem = pl.BlockSpec(memory_space=pltpu.VMEM), pl.BlockSpec(memory_space=pltpu.SMEM)
    hbm = pl.BlockSpec(memory_space=pl.ANY)
    bf16 = jnp.bfloat16
    strip = pltpu.VMEM((8, BLOCK, D), bf16)
    near = LONG + SHORT + 1

    dma = pltpu.SemaphoreType.DMA

    def many(count):
        return dma((count,))

    mixed, w_out_whole = pl.pallas_call(
        kernel,
        out_shape=(
            jax.ShapeDtypeStruct((fine_embed.shape[0], HD), bf16), jax.ShapeDtypeStruct((HD, D), bf16)
        ),
        in_specs=[vmem] * 4 + [smem, vmem, vmem] + [hbm, vmem, vmem],
        out_specs=(hbm, hbm),
        scratch_shapes=[
            pltpu.VMEM((4, 2, 3, NZ, 2, 48, 128), bf16),
            pltpu.VMEM((2, NZ, BLOCK, D), bf16),
            strip,
        ] + [strip] * (LONG + SHORT) + [
            pltpu.VMEM((near, BLOCK, D), bf16),
            pltpu.VMEM((6, BLOCK, D), bf16),
            pltpu.VMEM((6, BLOCK, D), bf16),
            pltpu.VMEM((512, D), bf16),
            pltpu.VMEM((512, D), bf16),
            pltpu.VMEM((256, D), bf16),
            pltpu.VMEM((512, HD), bf16),
            pltpu.VMEM((2, 256, 256), bf16),
            pltpu.VMEM((HEADS // 2, 512, 128), bf16),
            pltpu.VMEM((HD, D), bf16),
            pltpu.VMEM((2, 1, D), jnp.float32),
            pltpu.VMEM((NT, NT), jnp.int32),
            pltpu.SMEM((NT, NT), jnp.int32),
            dma, dma, many(HEADS // 2 + 1),
            dma, many(8),
            dma, many(2 * LONG),
            dma, dma,
            dma, dma,
            dma, dma,
            dma, many(9),
            dma, many(9),
            dma, many(9),
            dma, dma,
        ],
        compiler_params=pltpu.CompilerParams(
            collective_id=0, has_side_effects=True, vmem_limit_bytes=56 << 20
        ),
    )(coarse.reshape(8, BLOCK, D), w_query, w_kv, w_out, readers.T, readers.T, picks.T, fine_embed, fine_gain, coarse_gain)
    return jnp.dot(mixed, w_out_whole, preferred_element_type=jnp.float32).astype(bf16)


def solution(mesh):
    placed = (
        P(("img", "tile"), None),
        P(("img", "tile"), None),
        P(),
        P(),
        P("tile", None),
        P("tile", None),
        P("tile", None),
        P("img", None),
        P("img", None),
    )
    return jax.shard_map(
        body, mesh=mesh, in_specs=placed, out_specs=P(("img", "tile"), None), check_vma=False
    )
```

```python
import jax
import jax.numpy as jnp
from jax import lax
from jax.experimental import pallas as pl
from jax.experimental.pallas import tpu as pltpu
from jax.sharding import PartitionSpec as P

HEADS = 12
HDIM = 64
BLOCK = 16
NZ = 16
NT = 32
D = 1536
HD = 768
LONG = 5
SHORT = 4
EPSILON = 1e-06
LOG2E = 1.4426950408889634
MESH = pl.DeviceIdType.MESH


def wrap(value, size):
    return lax.rem(value + size, size)


def normalized(values, gain):
    inverse = lax.rsqrt(jnp.mean(values * values, axis=-1, keepdims=True) + EPSILON)
    return (values * inverse * gain).astype(jnp.bfloat16)


def kernel(
    coarse_ref, wq_ref, wkv_ref, wo_ref, readers_ref, reader_rows, pick_rows, fine_hbm, fine_gain_ref, coarse_gain_ref, mixed, w_out,
    w_ref, x_ref, up_ref, l1, l2, l3, l4, l5, s1, s2, s3, s4, stage, far_l, far_s,
    fine, fine_n, coarse_n, query, keyval, gains, blk_rows, blk,
    local_sem, blk_sem, zw_send, zw_recv, e_send, e_recv, c_send, c_recv, far_send, far_recv, near_send, near_recv, up_send, up_recv,
    a_send, a_recv, a2_send, a2_recv, b_send, b_recv, d_send, d_recv,
):
    img, tile = lax.axis_index("img"), lax.axis_index("tile")
    z, core = tile // 2, lax.rem(tile, 2)
    other = 1 - core
    sign = 1 - 2 * core
    gx, gy = img // 4, lax.rem(img, 4)
    a = jnp.where(core == 0, gx, gy)
    b = jnp.where(core == 0, gy, gx)
    bp = lax.rem(b, 2)

    fine_copy = pltpu.make_async_copy(fine_hbm, fine, local_sem)
    fine_copy.start()

    def along(steps):
        return wrap(z + sign * steps, NZ)

    def on_z(steps, which):
        return {"img": img, "tile": along(steps) * 2 + which}

    def on_plane(first, second):
        first, second = wrap(first, 4), wrap(second, 4)
        return {"img": jnp.where(core == 0, first * 4 + second, second * 4 + first), "tile": tile}

    sibling = {"img": img, "tile": z * 2 + other}
    a_up, a_down = on_plane(a + 1, b), on_plane(a - 1, b)
    b_up, b_down, twin = on_plane(a, b + 1), on_plane(a, b - 1), on_plane(a, lax.rem(b + 2, 4))
    ahead, behind = on_z(1, core), on_z(-1, core)

    partners = [sibling, a_up, a_down, b_up, b_down, twin]
    partners += [on_z(j, which) for j in (-3, -2, -1, 1, 2, 3) for which in (core, other)]
    barrier = pltpu.get_barrier_semaphore()
    for partner in partners:
        pl.semaphore_signal(barrier, inc=1, device_id=partner, device_id_type=MESH)

    for strip in range(NT):
        blk_rows[strip : strip + 1, :] = jnp.sum(
            jnp.where(reader_rows[...] == strip, pick_rows[...], 0), axis=0, keepdims=True
        )
    blk_copy = pltpu.make_async_copy(blk_rows, blk, blk_sem)
    blk_copy.start()

    piece_index = 2 * a + bp

    @pl.when(piece_index < 2)
    def _():
        for i in range(3):
            lanes = pl.ds(pl.multiple_of((3 * piece_index + i) * 128, 128), 128)
            w_ref[a, bp, i, z, core] = wq_ref[:, lanes]

    @pl.when((piece_index >= 2) & (piece_index < 6))
    def _():
        for i in range(3):
            lanes = pl.ds(pl.multiple_of((3 * piece_index + i - 6) * 128, 128), 128)
            w_ref[a, bp, i, z, core] = wkv_ref[:, lanes]

    @pl.when(piece_index >= 6)
    def _():
        for i in range(3):
            slab = 3 * piece_index + i - 18
            upper = wo_ref[:, pl.ds(pl.multiple_of(slab * 128, 128), 128)].astype(jnp.float32)
            lower = wo_ref[:, pl.ds(pl.multiple_of((slab + 6) * 128, 128), 128)].astype(jnp.float32)
            w_ref[a, bp, i, z, core] = jnp.concatenate([upper, lower], axis=0).astype(jnp.bfloat16)

    pl.semaphore_wait(barrier, len(partners))

    def remote(src, dst, send, recv, device):
        return pltpu.make_async_remote_copy(
            src_ref=src, dst_ref=dst, send_sem=send, recv_sem=recv, device_id=device, device_id_type=MESH
        )

    def go(copy):
        copy.start()

    def drain():
        for which in range(2):
            @pl.when(kind == which)
            def _():
                whole(shards(7 + which), zw_send, zw_recv.at[0]).wait_send()
                whole(shards(7 + which), e_send, e_recv.at[0]).wait_send()

        whole(w_ref.at[a, bp], a_send, a_recv.at[0]).wait_send()
        whole(shards(16), a2_send, a2_recv.at[0]).wait_send()
        whole(w_ref.at[:, bp, :, :, core], b_send, b_recv.at[0]).wait_send()
        whole(w_ref.at[:, :, :, :, core], d_send, d_recv).wait_send()
        whole(w_ref.at[pl.ds(0, 3), :, :, :, core], c_send, c_recv.at[0]).wait_send()
        whole(x_ref.at[0, pl.ds(0, LONG + SHORT + 1)], near_send, near_recv).wait_send()
        whole(x_ref.at[0, pl.ds(0, 12)], far_send, far_recv).wait_send()
        whole(up_ref.at[pl.ds(0, 4)], up_send, up_recv).wait_send()

    def place(m):
        return along(-m if m <= 8 else m - 8)

    def group(step):
        return [0] if step == 0 else [8] if step == 8 else [step, 8 + step]

    def whole(ref, send, recv):
        return remote(ref, ref, send, recv, sibling)

    def shards(count):
        return w_ref.at[a, bp, :, pl.ds(0, count), core]


    kind = lax.rem(a // 2 + b // 2, 2)
    onward = 1 - 2 * kind
    next_on_z = on_z(onward, core)

    def unless_last(step, which, act):
        if step < 8:
            act()
        else:
            pl.when(kind == which)(act)

    def zw_start(step):
        where = w_ref.at[a, bp, :, along(-onward * (step - 1)), core]
        unless_last(step, 1, remote(where, where, zw_send, zw_recv.at[step - 1], next_on_z).start)

    def twin_start(step):
        where = w_ref.at[a, bp, :, along(-onward * step), core]
        unless_last(step, 1, remote(where, where, e_send, e_recv.at[step - 1], twin).start)

    def x1_start(step):
        for m in group(step):
            where = w_ref.at[a, bp, :, place(m), core]
            for device in (a_up, a_down):
                go(remote(where, where, a_send, a_recv.at[step], device))

    def x2_start(step):
        for m in group(step):
            rising = m < 8
            where = w_ref.at[wrap(a - 1 if rising else a + 1, 4), bp, :, place(m), core]
            go(remote(where, where, a2_send, a2_recv.at[step], a_up if rising else a_down))

    def y_start(step):
        for m in group(step):
            where = w_ref.at[:, bp, :, place(m), core]
            go(remote(where, where, b_send, b_recv.at[step], b_up if m < 8 else b_down))
            go(remote(where, where, d_send, d_recv, sibling))

    def d2_start(step):
        for m in group(step):
            where = w_ref.at[:, 1 - bp, :, place(m), core]
            go(remote(where, where, d_send, d_recv, sibling))

    long_buf = [coarse_ref, l1, l2, l3, l4, l5]
    short_buf = [coarse_ref, s1, s2, s3, s4]

    def c_copy(step, half, forward):
        bufs = long_buf if forward else short_buf
        slot = 2 * (step - 1) + half
        part = pl.ds(4 * half, 4)
        return remote(
            bufs[step - 1].at[part], bufs[step].at[part], c_send, c_recv.at[slot],
            ahead if forward else behind,
        )

    def c_start(step, half):
        if step <= LONG:
            c_copy(step, half, True).start()
        if step <= SHORT:
            c_copy(step, half, False).start()

    def c_pass(step, half):
        blocks = 8 if step <= SHORT else 4
        whole(x_ref.at[0, pl.ds(0, blocks)], c_send, c_recv.at[2 * (step - 1) + half]).wait_recv()
        if step < LONG:
            c_start(step + 1, half)

    def share(buf, steps, index, distance):
        strip = along(steps) * 2 + core
        x_ref[core, distance] = buf[blk[strip, tile]]
        stage[index] = buf[blk[strip, z * 2 + other]]
        go(remote(stage.at[index], x_ref.at[core, distance], near_send, near_recv, sibling))
        if abs(steps) <= 3:
            position = lax.rem(z, 4) + sign * steps
            inside = (position >= 0) & (position < 4)
            column = lax.rem(tile, 8)
            column_other = lax.rem(z * 2 + other, 8)
            kept = jnp.clip(position, 0, 3)
            row = 2 * kept + core
            sent = remote(
                buf.at[column_other], up_ref.at[row], up_send, up_recv, sibling
            )

            @pl.when(inside)
            def _():
                up_ref[row] = buf[column]
                sent.start()


    def share_step(step):
        if step == 0:
            share(coarse_ref, 0, 0, 0)
            return
        if step <= LONG:
            share(long_buf[step], -step, step, step)
        if step <= SHORT:
            share(short_buf[step], step, LONG + step, NZ - step)

    def send_far(forward):
        buf = l5 if forward else s4
        held = LONG if forward else SHORT
        picked = far_l if forward else far_s
        strip = along(-LONG if forward else SHORT) * 2 + core
        for j in (3, 2, 1):
            target = along(j if forward else -j)
            distance = held + j if forward else NZ - held - j
            for e in range(2):
                which = core if e == 0 else other
                picked[2 * (j - 1) + e] = buf[blk[strip, target * 2 + which]]
                go(remote(
                    picked.at[2 * (j - 1) + e], x_ref.at[core, distance], far_send, far_recv,
                    {"img": img, "tile": target * 2 + which},
                ))

    def tick(i):
        if 1 <= i <= 8:
            unless_last(i, 1, whole(shards(1), zw_send, zw_recv.at[i - 1]).wait_recv)
        if i <= 7:
            zw_start(i + 1)
        if 1 <= i <= 8:
            twin_start(i)
        if 2 <= i <= 9:
            unless_last(i - 1, 0, whole(shards(1), e_send, e_recv.at[i - 2]).wait_recv)
        if 1 <= i <= 9:
            x1_start(i - 1)
        if 2 <= i <= 10:
            whole(shards(2 * len(group(i - 2))), a_send, a_recv.at[i - 2]).wait_recv()
            x2_start(i - 2)
        if 3 <= i <= 11:
            whole(shards(len(group(i - 3))), a2_send, a2_recv.at[i - 3]).wait_recv()
            y_start(i - 3)
        if 5 <= i <= 5 + 8:
            count = len(group(i - 5))
            whole(w_ref.at[:, bp, :, pl.ds(0, count), core], b_send, b_recv.at[i - 5]).wait_recv()
            d2_start(i - 5)

    c_start(1, 0)
    tick(0)
    c_start(1, 1)
    blk_copy.wait()
    tick(1)
    c_pass(1, 0)
    share_step(0)
    tick(2)
    c_pass(1, 1)
    tick(3)
    c_pass(2, 0)
    share_step(1)
    tick(4)
    c_pass(2, 1)
    tick(5)
    c_pass(3, 0)
    share_step(2)
    tick(6)
    c_pass(3, 1)
    tick(7)
    c_pass(4, 0)
    share_step(3)
    tick(8)

    for index, gain_ref in enumerate((fine_gain_ref, coarse_gain_ref)):
        gains[index] = gain_ref[...].reshape(1, D)
    fine_copy.wait()
    whole(up_ref.at[pl.ds(0, 4)], up_send, up_recv).wait_recv()

    rows = lax.broadcasted_iota(jnp.int32, (32, BLOCK), 0) // 2
    spread = (rows == lax.broadcasted_iota(jnp.int32, (32, BLOCK), 1)).astype(jnp.bfloat16)

    def fine_norm(first, last):
        @pl.loop(first, last)
        def _(i):
            up = jnp.dot(spread, up_ref[i], preferred_element_type=jnp.float32)
            for half in range(2):
                part = pl.ds(pl.multiple_of(i * 64 + half * 32, 32), 32)
                hidden = fine[part, :].astype(jnp.float32) + up
                fine_n[part, :] = normalized(hidden, gains[0])

    def slab(index):
        return w_ref[index // 6, lax.rem(index // 3, 2), lax.rem(index, 3)].reshape(D, 128)

    def project_query():
        @pl.loop(0, 3)
        def _(j):
            pair = jnp.concatenate([slab(2 * j), slab(2 * j + 1)], axis=1)
            query[:, pl.ds(pl.multiple_of(j * 256, 256), 256)] = jnp.dot(
                fine_n[...], pair, preferred_element_type=jnp.float32
            ).astype(jnp.bfloat16)

    def order_out():
        @pl.loop(0, NZ)
        def _(k):
            part = pl.ds(pl.multiple_of(k * 48, 48), 48)
            for j in range(6):
                even = w_ref[3, j // 3, j % 3, k, 0].astype(jnp.float32)
                odd = w_ref[3, j // 3, j % 3, k, 1].astype(jnp.float32)
                for half in range(2):
                    cut = slice(24 * half, 24 * half + 24)
                    w_out[part, pl.ds((j + 6 * half) * 128, 128)] = jnp.concatenate(
                        [even[cut], odd[cut]], axis=0
                    ).astype(jnp.bfloat16)

    c_pass(4, 1)
    send_far(False)
    tick(9)
    fine_norm(0, 4)
    tick(10)
    c_pass(5, 0)
    tick(11)
    c_pass(5, 1)
    send_far(True)
    share_step(4)
    share_step(5)
    fine_norm(4, 8)
    tick(12)
    tick(13)
    whole(w_ref.at[:, :, :, :, core], d_send, d_recv).wait_recv()
    project_query()
    order_out()
    drain()
    whole(x_ref.at[0, pl.ds(0, LONG + SHORT + 1)], near_send, near_recv).wait_recv()
    whole(x_ref.at[0, pl.ds(0, 12)], far_send, far_recv).wait_recv()

    @pl.loop(0, 16, unroll=4)
    def _(r):
        reader = readers_ref[r, tile]
        lane = lax.rem(reader, 2)
        distance = lax.rem((z - reader // 2) * (1 - 2 * lane) + NZ, NZ)
        values = x_ref[lane, distance].astype(jnp.float32)
        coarse_n[pl.ds(pl.multiple_of(r * BLOCK, BLOCK), BLOCK), :] = normalized(values, gains[1])

    def projected(p):
        pair = jnp.concatenate([slab(6 + p), slab(12 + p)], axis=1)
        return jnp.dot(coarse_n[...], pair, preferred_element_type=jnp.float32).astype(jnp.bfloat16)

    low = lax.broadcasted_iota(jnp.int32, (1, 128), 1) < HDIM
    keyval[0] = projected(0)

    @pl.loop(0, HEADS // 2, unroll=2)
    def _(p):
        lanes = pl.ds(pl.multiple_of(p * 128, 128), 128)
        both = keyval[lax.rem(p, 2)]
        keyval[lax.rem(p + 1, 2)] = projected(jnp.minimum(p + 1, HEADS // 2 - 1))
        keys, values = both[:, :128], both[:, 128:]
        zero, one = jnp.zeros_like(keys), jnp.ones_like(values)
        key_pair = [jnp.where(low, keys, zero), jnp.where(low, zero, keys)]
        value_pair = [jnp.where(low, values, one), jnp.where(low, one, values)]
        queries = query[:, lanes]
        results = []
        for h in range(2):
            scores = lax.dot_general(
                queries, key_pair[h], (((1,), (1,)), ((), ())), preferred_element_type=jnp.float32
            )
            top = jnp.max(scores, axis=-1, keepdims=True)
            exponent = jnp.exp2((scores - top) * (HDIM ** (-0.5) * LOG2E)).astype(jnp.bfloat16)
            results.append(jnp.dot(exponent, value_pair[h], preferred_element_type=jnp.float32))
        total = pltpu.roll(jnp.where(low, results[1], results[0]), HDIM, 1)
        mixed[:, lanes] = (jnp.where(low, results[0], results[1]) / total).astype(jnp.bfloat16)


def body(coarse, fine_embed, fine_gain, coarse_gain, w_query, w_kv, w_out, readers, picks):
    vmem, smem = pl.BlockSpec(memory_space=pltpu.VMEM), pl.BlockSpec(memory_space=pltpu.SMEM)
    hbm = pl.BlockSpec(memory_space=pl.ANY)
    bf16 = jnp.bfloat16
    strip = pltpu.VMEM((8, BLOCK, D), bf16)
    near = LONG + SHORT + 1

    dma = pltpu.SemaphoreType.DMA

    def many(count):
        return dma((count,))

    mixed, w_out_whole = pl.pallas_call(
        kernel,
        out_shape=(
            pltpu.VMEM((fine_embed.shape[0], HD), bf16), pltpu.VMEM((HD, D), bf16)
        ),
        in_specs=[vmem] * 4 + [smem, vmem, vmem] + [hbm, vmem, vmem],
        out_specs=(vmem, vmem),
        scratch_shapes=[
            pltpu.VMEM((4, 2, 3, NZ, 2, 48, 128), bf16),
            pltpu.VMEM((2, NZ, BLOCK, D), bf16),
            strip,
        ] + [strip] * (LONG + SHORT) + [
            pltpu.VMEM((near, BLOCK, D), bf16),
            pltpu.VMEM((6, BLOCK, D), bf16),
            pltpu.VMEM((6, BLOCK, D), bf16),
            pltpu.VMEM((512, D), bf16),
            pltpu.VMEM((512, D), bf16),
            pltpu.VMEM((256, D), bf16),
            pltpu.VMEM((512, HD), bf16),
            pltpu.VMEM((2, 256, 256), bf16),
            pltpu.VMEM((2, 1, D), jnp.float32),
            pltpu.VMEM((NT, NT), jnp.int32),
            pltpu.SMEM((NT, NT), jnp.int32),
            dma, dma,
            dma, many(8),
            dma, many(8),
            dma, many(2 * LONG),
            dma, dma,
            dma, dma,
            dma, dma,
            dma, many(9),
            dma, many(9),
            dma, many(9),
            dma, dma,
        ],
        compiler_params=pltpu.CompilerParams(
            collective_id=0, has_side_effects=True, vmem_limit_bytes=40 << 20
        ),
    )(*(pltpu.with_memory_space_constraint(operand, pltpu.HBM) for operand in (
        coarse.reshape(8, BLOCK, D), w_query, w_kv, w_out, readers.T, readers.T, picks.T, fine_embed, fine_gain,
        coarse_gain,
    )))
    return jnp.dot(mixed, w_out_whole, preferred_element_type=jnp.float32).astype(bf16)


def solution(mesh):
    placed = (
        P(("img", "tile"), None),
        P(("img", "tile"), None),
        P(),
        P(),
        P("tile", None),
        P("tile", None),
        P("tile", None),
        P("img", None),
        P("img", None),
    )
    return jax.shard_map(
        body, mesh=mesh, in_specs=placed, out_specs=P(("img", "tile"), None), check_vma=False
    )
```

```python
import jax
import jax.numpy as jnp
from jax import lax
from jax.experimental import pallas as pl
from jax.experimental.pallas import tpu as pltpu
from jax.sharding import PartitionSpec as P

HEADS = 12
HDIM = 64
BLOCK = 16
NZ = 16
NT = 32
D = 1536
HD = 768
LONG = 5
SHORT = 4
EPSILON = 1e-06
LOG2E = 1.4426950408889634
MESH = pl.DeviceIdType.MESH


def wrap(value, size):
    return lax.rem(value + size, size)


def normalized(values, gain):
    inverse = lax.rsqrt(jnp.mean(values * values, axis=-1, keepdims=True) + EPSILON)
    return (values * inverse * gain).astype(jnp.bfloat16)


def kernel(
    coarse_ref, wq_ref, wkv_ref, wo_ref, readers_ref, reader_rows, pick_rows, fine_hbm, fine_gain_ref, coarse_gain_ref, mixed, w_out,
    w_ref, x_ref, up_ref, l1, l2, l3, l4, l5, s1, s2, s3, s4, stage, far_l, far_s,
    fine, fine_n, coarse_n, query, keyval, gains, blk_rows, blk,
    local_sem, blk_sem, zw_send, zw_recv, e_send, e_recv, c_send, c_recv, far_send, far_recv, near_send, near_recv, up_send, up_recv,
    a_send, a_recv, a2_send, a2_recv, b_send, b_recv, d_send, d_recv,
):
    img, tile = lax.axis_index("img"), lax.axis_index("tile")
    z, core = tile // 2, lax.rem(tile, 2)
    other = 1 - core
    sign = 1 - 2 * core
    gx, gy = img // 4, lax.rem(img, 4)
    a = jnp.where(core == 0, gx, gy)
    b = jnp.where(core == 0, gy, gx)
    bp = lax.rem(b, 2)

    fine_copy = pltpu.make_async_copy(fine_hbm, fine, local_sem)
    fine_copy.start()

    def along(steps):
        return wrap(z + sign * steps, NZ)

    def on_z(steps, which):
        return {"img": img, "tile": along(steps) * 2 + which}

    def on_plane(first, second):
        first, second = wrap(first, 4), wrap(second, 4)
        return {"img": jnp.where(core == 0, first * 4 + second, second * 4 + first), "tile": tile}

    sibling = {"img": img, "tile": z * 2 + other}
    a_up, a_down = on_plane(a + 1, b), on_plane(a - 1, b)
    b_up, b_down, twin = on_plane(a, b + 1), on_plane(a, b - 1), on_plane(a, lax.rem(b + 2, 4))
    ahead, behind = on_z(1, core), on_z(-1, core)

    partners = [sibling, a_up, a_down, b_up, b_down, twin]
    partners += [on_z(j, which) for j in (-3, -2, -1, 1, 2, 3) for which in (core, other)]
    barrier = pltpu.get_barrier_semaphore()
    for partner in partners:
        pl.semaphore_signal(barrier, inc=1, device_id=partner, device_id_type=MESH)

    piece_index = 2 * a + bp

    @pl.when(piece_index < 2)
    def _():
        for i in range(3):
            lanes = pl.ds(pl.multiple_of((3 * piece_index + i) * 128, 128), 128)
            w_ref[a, bp, i, z, core] = wq_ref[:, lanes]

    @pl.when((piece_index >= 2) & (piece_index < 6))
    def _():
        for i in range(3):
            lanes = pl.ds(pl.multiple_of((3 * piece_index + i - 6) * 128, 128), 128)
            w_ref[a, bp, i, z, core] = wkv_ref[:, lanes]

    @pl.when(piece_index >= 6)
    def _():
        for i in range(3):
            slab = 3 * piece_index + i - 18
            upper = wo_ref[:, pl.ds(pl.multiple_of(slab * 128, 128), 128)].astype(jnp.float32)
            lower = wo_ref[:, pl.ds(pl.multiple_of((slab + 6) * 128, 128), 128)].astype(jnp.float32)
            w_ref[a, bp, i, z, core] = jnp.concatenate([upper, lower], axis=0).astype(jnp.bfloat16)

    pl.semaphore_wait(barrier, len(partners))

    def remote(src, dst, send, recv, device):
        return pltpu.make_async_remote_copy(
            src_ref=src, dst_ref=dst, send_sem=send, recv_sem=recv, device_id=device, device_id_type=MESH
        )

    def go(copy):
        copy.start()

    def drain():
        for which in range(2):
            @pl.when(kind == which)
            def _():
                whole(shards(7 + which), zw_send, zw_recv.at[0]).wait_send()
                whole(shards(7 + which), e_send, e_recv.at[0]).wait_send()

        whole(w_ref.at[a, bp], a_send, a_recv.at[0]).wait_send()
        whole(shards(16), a2_send, a2_recv.at[0]).wait_send()
        whole(w_ref.at[:, bp, :, :, core], b_send, b_recv.at[0]).wait_send()
        whole(w_ref.at[:, :, :, :, core], d_send, d_recv).wait_send()
        whole(w_ref.at[pl.ds(0, 3), :, :, :, core], c_send, c_recv.at[0]).wait_send()
        whole(x_ref.at[0, pl.ds(0, LONG + SHORT + 1)], near_send, near_recv).wait_send()
        whole(x_ref.at[0, pl.ds(0, 12)], far_send, far_recv).wait_send()
        whole(up_ref.at[pl.ds(0, 4)], up_send, up_recv).wait_send()

    def place(m):
        return along(-m if m <= 8 else m - 8)

    def group(step):
        return [0] if step == 0 else [8] if step == 8 else [step, 8 + step]

    def whole(ref, send, recv):
        return remote(ref, ref, send, recv, sibling)

    def shards(count):
        return w_ref.at[a, bp, :, pl.ds(0, count), core]


    kind = lax.rem(a // 2 + b // 2, 2)
    onward = 1 - 2 * kind

    def unless_last(step, which, act):
        if step < 8:
            act()
        else:
            pl.when(kind == which)(act)

    def zw_start(step):
        stride = 1 if step == 1 else 2
        where = w_ref.at[a, bp, :, along(-onward * (step - stride)), core]
        unless_last(step, 1, remote(where, where, zw_send, zw_recv.at[step - 1], on_z(stride * onward, core)).start)

    def twin_start(step):
        where = w_ref.at[a, bp, :, along(-onward * step), core]
        unless_last(step, 1, remote(where, where, e_send, e_recv.at[step - 1], twin).start)

    def x1_start(step):
        for m in group(step):
            where = w_ref.at[a, bp, :, place(m), core]
            for device in (a_up, a_down):
                go(remote(where, where, a_send, a_recv.at[step], device))

    def x2_start(step):
        for m in group(step):
            rising = m < 8
            where = w_ref.at[wrap(a - 1 if rising else a + 1, 4), bp, :, place(m), core]
            go(remote(where, where, a2_send, a2_recv.at[step], a_up if rising else a_down))

    def y_start(step):
        for m in group(step):
            where = w_ref.at[:, bp, :, place(m), core]
            go(remote(where, where, b_send, b_recv.at[step], b_up if m < 8 else b_down))
            go(remote(where, where, d_send, d_recv, sibling))

    def d2_start(step):
        for m in group(step):
            where = w_ref.at[:, 1 - bp, :, place(m), core]
            go(remote(where, where, d_send, d_recv, sibling))

    long_buf = [coarse_ref, l1, l2, l3, l4, l5]
    short_buf = [coarse_ref, s1, s2, s3, s4]

    def c_copy(step, half, forward):
        bufs = long_buf if forward else short_buf
        slot = 2 * (step - 1) + half
        part = pl.ds(4 * half, 4)
        return remote(
            bufs[step - 1].at[part], bufs[step].at[part], c_send, c_recv.at[slot],
            ahead if forward else behind,
        )

    def c_start(step, half):
        if step <= LONG:
            c_copy(step, half, True).start()
        if step <= SHORT:
            c_copy(step, half, False).start()

    def c_pass(step, half):
        blocks = 8 if step <= SHORT else 4
        whole(x_ref.at[0, pl.ds(0, blocks)], c_send, c_recv.at[2 * (step - 1) + half]).wait_recv()
        if step < LONG:
            c_start(step + 1, half)

    def share(buf, steps, index, distance):
        strip = along(steps) * 2 + core
        x_ref[core, distance] = normalized(buf[blk[strip, tile]].astype(jnp.float32), gains[1])
        stage[index] = normalized(buf[blk[strip, z * 2 + other]].astype(jnp.float32), gains[1])
        go(remote(stage.at[index], x_ref.at[core, distance], near_send, near_recv, sibling))
        if abs(steps) <= 3:
            position = lax.rem(z, 4) + sign * steps
            inside = (position >= 0) & (position < 4)
            column = lax.rem(tile, 8)
            column_other = lax.rem(z * 2 + other, 8)
            kept = jnp.clip(position, 0, 3)
            row = 2 * kept + core
            sent = remote(
                buf.at[column_other], up_ref.at[row], up_send, up_recv, sibling
            )

            @pl.when(inside)
            def _():
                up_ref[row] = buf[column]
                sent.start()


    def share_step(step):
        if step == 0:
            share(coarse_ref, 0, 0, 0)
            return
        if step <= LONG:
            share(long_buf[step], -step, step, step)
        if step <= SHORT:
            share(short_buf[step], step, LONG + step, NZ - step)

    def send_far(forward):
        buf = l5 if forward else s4
        held = LONG if forward else SHORT
        picked = far_l if forward else far_s
        strip = along(-LONG if forward else SHORT) * 2 + core
        for j in (3, 2, 1):
            target = along(j if forward else -j)
            distance = held + j if forward else NZ - held - j
            for e in range(2):
                which = core if e == 0 else other
                picked[2 * (j - 1) + e] = normalized(buf[blk[strip, target * 2 + which]].astype(jnp.float32), gains[1])
                go(remote(
                    picked.at[2 * (j - 1) + e], x_ref.at[core, distance], far_send, far_recv,
                    {"img": img, "tile": target * 2 + which},
                ))

    def tick(i):
        if 1 <= i <= 8:
            unless_last(i, 1, whole(shards(1), zw_send, zw_recv.at[i - 1]).wait_recv)
        if i == 0:
            zw_start(1)
        if i <= 6:
            zw_start(i + 2)
        if 1 <= i <= 8:
            twin_start(i)
        if 2 <= i <= 9:
            unless_last(i - 1, 0, whole(shards(1), e_send, e_recv.at[i - 2]).wait_recv)
        if 1 <= i <= 9:
            x1_start(i - 1)
        if 2 <= i <= 10:
            whole(shards(2 * len(group(i - 2))), a_send, a_recv.at[i - 2]).wait_recv()
            x2_start(i - 2)
        if 3 <= i <= 11:
            whole(shards(len(group(i - 3))), a2_send, a2_recv.at[i - 3]).wait_recv()
            y_start(i - 3)
        if 5 <= i <= 5 + 8:
            count = len(group(i - 5))
            whole(w_ref.at[:, bp, :, pl.ds(0, count), core], b_send, b_recv.at[i - 5]).wait_recv()
            d2_start(i - 5)

    c_start(1, 0)
    tick(0)
    c_start(1, 1)
    for strip in range(NT):
        blk_rows[strip : strip + 1, :] = jnp.sum(
            jnp.where(reader_rows[...] == strip, pick_rows[...], 0), axis=0, keepdims=True
        )
    blk_copy = pltpu.make_async_copy(blk_rows, blk, blk_sem)
    blk_copy.start()

    tick(1)
    c_pass(1, 0)
    blk_copy.wait()
    for index, gain_ref in enumerate((fine_gain_ref, coarse_gain_ref)):
        gains[index] = gain_ref[...].reshape(1, D)
    share_step(0)
    tick(2)
    c_pass(1, 1)
    tick(3)
    c_pass(2, 0)
    share_step(1)
    tick(4)
    c_pass(2, 1)
    tick(5)
    c_pass(3, 0)
    share_step(2)
    tick(6)
    c_pass(3, 1)
    tick(7)
    c_pass(4, 0)
    share_step(3)
    tick(8)

    fine_copy.wait()
    whole(up_ref.at[pl.ds(0, 4)], up_send, up_recv).wait_recv()

    rows = lax.broadcasted_iota(jnp.int32, (32, BLOCK), 0) // 2
    spread = (rows == lax.broadcasted_iota(jnp.int32, (32, BLOCK), 1)).astype(jnp.bfloat16)

    def fine_norm(first, last):
        @pl.loop(first, last)
        def _(i):
            up = jnp.dot(spread, up_ref[i], preferred_element_type=jnp.float32)
            for half in range(2):
                part = pl.ds(pl.multiple_of(i * 64 + half * 32, 32), 32)
                hidden = fine[part, :].astype(jnp.float32) + up
                fine_n[part, :] = normalized(hidden, gains[0])

    def slab(index):
        return w_ref[index // 6, lax.rem(index // 3, 2), lax.rem(index, 3)].reshape(D, 128)

    def project_query():
        @pl.loop(0, 3)
        def _(j):
            pair = jnp.concatenate([slab(2 * j), slab(2 * j + 1)], axis=1)
            query[:, pl.ds(pl.multiple_of(j * 256, 256), 256)] = jnp.dot(
                fine_n[...], pair, preferred_element_type=jnp.float32
            ).astype(jnp.bfloat16)

    def order_out():
        @pl.loop(0, NZ)
        def _(k):
            part = pl.ds(pl.multiple_of(k * 48, 48), 48)
            for j in range(6):
                even = w_ref[3, j // 3, j % 3, k, 0].astype(jnp.float32)
                odd = w_ref[3, j // 3, j % 3, k, 1].astype(jnp.float32)
                for half in range(2):
                    cut = slice(24 * half, 24 * half + 24)
                    w_out[part, pl.ds((j + 6 * half) * 128, 128)] = jnp.concatenate(
                        [even[cut], odd[cut]], axis=0
                    ).astype(jnp.bfloat16)

    c_pass(4, 1)
    send_far(False)
    tick(9)
    fine_norm(0, 4)
    tick(10)
    c_pass(5, 0)
    tick(11)
    c_pass(5, 1)
    send_far(True)
    share_step(4)
    share_step(5)
    fine_norm(4, 8)
    tick(12)
    tick(13)
    whole(w_ref.at[:, :, :, :, core], d_send, d_recv).wait_recv()
    project_query()
    order_out()
    whole(x_ref.at[0, pl.ds(0, LONG + SHORT + 1)], near_send, near_recv).wait_recv()
    whole(x_ref.at[0, pl.ds(0, 12)], far_send, far_recv).wait_recv()

    @pl.loop(0, 16, unroll=4)
    def _(r):
        reader = readers_ref[r, tile]
        lane = lax.rem(reader, 2)
        distance = lax.rem((z - reader // 2) * (1 - 2 * lane) + NZ, NZ)
        coarse_n[pl.ds(pl.multiple_of(r * BLOCK, BLOCK), BLOCK), :] = x_ref[lane, distance]

    def projected(p):
        pair = jnp.concatenate([slab(6 + p), slab(12 + p)], axis=1)
        return jnp.dot(coarse_n[...], pair, preferred_element_type=jnp.float32).astype(jnp.bfloat16)

    low = lax.broadcasted_iota(jnp.int32, (1, 128), 1) < HDIM
    keyval[0] = projected(0)

    @pl.loop(0, HEADS // 2, unroll=6)
    def _(p):
        lanes = pl.ds(pl.multiple_of(p * 128, 128), 128)
        both = keyval[lax.rem(p, 2)]
        keyval[lax.rem(p + 1, 2)] = projected(jnp.minimum(p + 1, HEADS // 2 - 1))
        keys, values = both[:, :128], both[:, 128:]
        zero, one = jnp.zeros_like(keys), jnp.ones_like(values)
        key_pair = [jnp.where(low, keys, zero), jnp.where(low, zero, keys)]
        value_pair = [jnp.where(low, values, one), jnp.where(low, one, values)]
        queries = query[:, lanes]
        results = []
        for h in range(2):
            scores = lax.dot_general(
                queries, key_pair[h], (((1,), (1,)), ((), ())), preferred_element_type=jnp.float32
            )
            top = jnp.max(scores, axis=-1, keepdims=True)
            exponent = jnp.exp2((scores - top) * (HDIM ** (-0.5) * LOG2E)).astype(jnp.bfloat16)
            results.append(jnp.dot(exponent, value_pair[h], preferred_element_type=jnp.float32))
        total = pltpu.roll(jnp.where(low, results[1], results[0]), HDIM, 1)
        mixed[:, lanes] = (jnp.where(low, results[0], results[1]) / total).astype(jnp.bfloat16)

    drain()


def body(coarse, fine_embed, fine_gain, coarse_gain, w_query, w_kv, w_out, readers, picks):
    vmem, smem = pl.BlockSpec(memory_space=pltpu.VMEM), pl.BlockSpec(memory_space=pltpu.SMEM)
    hbm = pl.BlockSpec(memory_space=pl.ANY)
    bf16 = jnp.bfloat16
    strip = pltpu.VMEM((8, BLOCK, D), bf16)
    near = LONG + SHORT + 1

    dma = pltpu.SemaphoreType.DMA

    def many(count):
        return dma((count,))

    mixed, w_out_whole = pl.pallas_call(
        kernel,
        out_shape=(
            pltpu.VMEM((fine_embed.shape[0], HD), bf16), pltpu.VMEM((HD, D), bf16)
        ),
        in_specs=[vmem] * 4 + [smem, vmem, vmem] + [hbm, vmem, vmem],
        out_specs=(vmem, vmem),
        scratch_shapes=[
            pltpu.VMEM((4, 2, 3, NZ, 2, 48, 128), bf16),
            pltpu.VMEM((2, NZ, BLOCK, D), bf16),
            strip,
        ] + [strip] * (LONG + SHORT) + [
            pltpu.VMEM((near, BLOCK, D), bf16),
            pltpu.VMEM((6, BLOCK, D), bf16),
            pltpu.VMEM((6, BLOCK, D), bf16),
            pltpu.VMEM((512, D), bf16),
            pltpu.VMEM((512, D), bf16),
            pltpu.VMEM((256, D), bf16),
            pltpu.VMEM((512, HD), bf16),
            pltpu.VMEM((2, 256, 256), bf16),
            pltpu.VMEM((2, 1, D), jnp.float32),
            pltpu.VMEM((NT, NT), jnp.int32),
            pltpu.SMEM((NT, NT), jnp.int32),
            dma, dma,
            dma, many(8),
            dma, many(8),
            dma, many(2 * LONG),
            dma, dma,
            dma, dma,
            dma, dma,
            dma, many(9),
            dma, many(9),
            dma, many(9),
            dma, dma,
        ],
        compiler_params=pltpu.CompilerParams(
            collective_id=0, has_side_effects=True, vmem_limit_bytes=40 << 20
        ),
    )(*(pltpu.with_memory_space_constraint(operand, pltpu.HBM) for operand in (
        coarse.reshape(8, BLOCK, D), w_query, w_kv, w_out, readers.T, readers.T, picks.T, fine_embed, fine_gain,
        coarse_gain,
    )))
    return jnp.dot(mixed, w_out_whole, preferred_element_type=jnp.float32).astype(bf16)


def solution(mesh):
    placed = (
        P(("img", "tile"), None),
        P(("img", "tile"), None),
        P(),
        P(),
        P("tile", None),
        P("tile", None),
        P("tile", None),
        P("img", None),
        P("img", None),
    )
    return jax.shard_map(
        body, mesh=mesh, in_specs=placed, out_specs=P(("img", "tile"), None), check_vma=False
    )
```

```python
import jax
import jax.numpy as jnp
from jax import lax
from jax.experimental import pallas as pl
from jax.experimental.pallas import tpu as pltpu
from jax.sharding import PartitionSpec as P

HEADS = 12
HDIM = 64
BLOCK = 16
NZ = 16
NT = 32
D = 1536
HD = 768
LONG = 5
SHORT = 4
EPSILON = 1e-06
LOG2E = 1.4426950408889634
MESH = pl.DeviceIdType.MESH


def wrap(value, size):
    return lax.rem(value + size, size)


def normalized(values, gain):
    inverse = lax.rsqrt(jnp.mean(values * values, axis=-1, keepdims=True) + EPSILON)
    return (values * inverse * gain).astype(jnp.bfloat16)


def kernel(
    coarse_ref, wq_ref, wkv_ref, wo_ref, readers_ref, reader_rows, pick_rows, fine_hbm, fine_gain_ref, coarse_gain_ref, mixed, w_out,
    w_ref, x_ref, up_ref, l1, l2, l3, l4, l5, s1, s2, s3, s4, stage, far_l, far_s,
    fine, fine_n, coarse_n, query, keyval, gains, blk_rows, blk,
    local_sem, blk_sem, zw_send, zw_recv, e_send, e_recv, c_send, c_recv, far_send, far_recv, near_send, near_recv, up_send, up_recv,
    a_send, a_recv, a2_send, a2_recv, b_send, b_recv, d_send, d_recv,
):
    img, tile = lax.axis_index("img"), lax.axis_index("tile")
    z, core = tile // 2, lax.rem(tile, 2)
    other = 1 - core
    sign = 1 - 2 * core
    gx, gy = img // 4, lax.rem(img, 4)
    a = jnp.where(core == 0, gx, gy)
    b = jnp.where(core == 0, gy, gx)
    bp = lax.rem(b, 2)

    fine_copy = pltpu.make_async_copy(fine_hbm, fine, local_sem)
    fine_copy.start()

    def along(steps):
        return wrap(z + sign * steps, NZ)

    def on_z(steps, which):
        return {"img": img, "tile": along(steps) * 2 + which}

    def on_plane(first, second):
        first, second = wrap(first, 4), wrap(second, 4)
        return {"img": jnp.where(core == 0, first * 4 + second, second * 4 + first), "tile": tile}

    sibling = {"img": img, "tile": z * 2 + other}
    a_up, a_down = on_plane(a + 1, b), on_plane(a - 1, b)
    b_up, b_down, twin = on_plane(a, b + 1), on_plane(a, b - 1), on_plane(a, lax.rem(b + 2, 4))
    ahead, behind = on_z(1, core), on_z(-1, core)

    partners = [sibling, a_up, a_down, b_up, b_down, twin]
    partners += [on_z(j, which) for j in (-3, -2, -1, 1, 2, 3) for which in (core, other)]
    barrier = pltpu.get_barrier_semaphore()
    for partner in partners:
        pl.semaphore_signal(barrier, inc=1, device_id=partner, device_id_type=MESH)

    piece_index = 2 * a + bp

    @pl.when(piece_index < 2)
    def _():
        for i in range(3):
            lanes = pl.ds(pl.multiple_of((3 * piece_index + i) * 128, 128), 128)
            w_ref[a, bp, i, z, core] = wq_ref[:, lanes]

    @pl.when((piece_index >= 2) & (piece_index < 6))
    def _():
        for i in range(3):
            lanes = pl.ds(pl.multiple_of((3 * piece_index + i - 6) * 128, 128), 128)
            w_ref[a, bp, i, z, core] = wkv_ref[:, lanes]

    @pl.when(piece_index >= 6)
    def _():
        for i in range(3):
            slab = 3 * piece_index + i - 18
            upper = wo_ref[:, pl.ds(pl.multiple_of(slab * 128, 128), 128)].astype(jnp.float32)
            lower = wo_ref[:, pl.ds(pl.multiple_of((slab + 6) * 128, 128), 128)].astype(jnp.float32)
            w_ref[a, bp, i, z, core] = jnp.concatenate([upper, lower], axis=0).astype(jnp.bfloat16)

    pl.semaphore_wait(barrier, len(partners))

    def remote(src, dst, send, recv, device):
        return pltpu.make_async_remote_copy(
            src_ref=src, dst_ref=dst, send_sem=send, recv_sem=recv, device_id=device, device_id_type=MESH
        )

    def go(copy):
        copy.start()

    def drain():
        for which in range(2):
            @pl.when(kind == which)
            def _():
                whole(shards(7 + which), zw_send, zw_recv.at[0]).wait_send()
                whole(shards(7 + which), e_send, e_recv.at[0]).wait_send()

        whole(w_ref.at[a, bp], a_send, a_recv.at[0]).wait_send()
        whole(shards(16), a2_send, a2_recv.at[0]).wait_send()
        whole(w_ref.at[:, bp, :, :, core], b_send, b_recv.at[0]).wait_send()
        whole(w_ref.at[:, :, :, :, core], d_send, d_recv).wait_send()
        whole(w_ref.at[pl.ds(0, 3), :, :, :, core], c_send, c_recv.at[0]).wait_send()
        whole(x_ref.at[0, pl.ds(0, LONG + SHORT + 1)], near_send, near_recv).wait_send()
        whole(x_ref.at[0, pl.ds(0, 12)], far_send, far_recv).wait_send()
        whole(up_ref.at[pl.ds(0, 4)], up_send, up_recv).wait_send()

    def place(m):
        return along(-m if m <= 8 else m - 8)

    def group(step):
        return [0] if step == 0 else [8] if step == 8 else [step, 8 + step]

    def whole(ref, send, recv):
        return remote(ref, ref, send, recv, sibling)

    def shards(count):
        return w_ref.at[a, bp, :, pl.ds(0, count), core]


    kind = lax.rem(a // 2 + b // 2, 2)
    onward = 1 - 2 * kind

    def unless_last(step, which, act):
        if step < 8:
            act()
        else:
            pl.when(kind == which)(act)

    def zw_start(step):
        stride = 1 if step == 1 else 2
        where = w_ref.at[a, bp, :, along(-onward * (step - stride)), core]
        unless_last(step, 1, remote(where, where, zw_send, zw_recv.at[step - 1], on_z(stride * onward, core)).start)

    def twin_start(step):
        where = w_ref.at[a, bp, :, along(-onward * step), core]
        unless_last(step, 1, remote(where, where, e_send, e_recv.at[step - 1], twin).start)

    def x1_start(step):
        for m in group(step):
            where = w_ref.at[a, bp, :, place(m), core]
            for device in (a_up, a_down):
                go(remote(where, where, a_send, a_recv.at[step], device))

    def x2_start(step):
        for m in group(step):
            rising = m < 8
            where = w_ref.at[wrap(a - 1 if rising else a + 1, 4), bp, :, place(m), core]
            go(remote(where, where, a2_send, a2_recv.at[step], a_up if rising else a_down))

    def y_start(step):
        for m in group(step):
            where = w_ref.at[:, bp, :, place(m), core]
            go(remote(where, where, b_send, b_recv.at[step], b_up if m < 8 else b_down))
            go(remote(where, where, d_send, d_recv, sibling))

    def d2_start(step):
        for m in group(step):
            where = w_ref.at[:, 1 - bp, :, place(m), core]
            go(remote(where, where, d_send, d_recv, sibling))

    long_buf = [coarse_ref, l1, l2, l3, l4, l5]
    short_buf = [coarse_ref, s1, s2, s3, s4]

    def c_copy(step, half, forward):
        bufs = long_buf if forward else short_buf
        slot = 2 * (step - 1) + half
        part = pl.ds(4 * half, 4)
        return remote(
            bufs[step - 1].at[part], bufs[step].at[part], c_send, c_recv.at[slot],
            ahead if forward else behind,
        )

    def c_start(step, half):
        if step <= LONG:
            c_copy(step, half, True).start()
        if step <= SHORT:
            c_copy(step, half, False).start()

    def c_pass(step, half):
        blocks = 8 if step <= SHORT else 4
        whole(x_ref.at[0, pl.ds(0, blocks)], c_send, c_recv.at[2 * (step - 1) + half]).wait_recv()
        if step < LONG:
            c_start(step + 1, half)

    def share(buf, steps, index, distance):
        strip = along(steps) * 2 + core
        x_ref[core, distance] = normalized(buf[blk[strip, tile]].astype(jnp.float32), gains[1])
        stage[index] = normalized(buf[blk[strip, z * 2 + other]].astype(jnp.float32), gains[1])
        go(remote(stage.at[index], x_ref.at[core, distance], near_send, near_recv, sibling))
        if abs(steps) <= 3:
            position = lax.rem(z, 4) + sign * steps
            inside = (position >= 0) & (position < 4)
            column = lax.rem(tile, 8)
            column_other = lax.rem(z * 2 + other, 8)
            kept = jnp.clip(position, 0, 3)
            row = 2 * kept + core
            sent = remote(
                buf.at[column_other], up_ref.at[row], up_send, up_recv, sibling
            )

            @pl.when(inside)
            def _():
                up_ref[row] = buf[column]
                sent.start()


    def share_step(step):
        if step == 0:
            share(coarse_ref, 0, 0, 0)
            return
        if step <= LONG:
            share(long_buf[step], -step, step, step)
        if step <= SHORT:
            share(short_buf[step], step, LONG + step, NZ - step)

    def send_far(forward):
        buf = l5 if forward else s4
        held = LONG if forward else SHORT
        picked = far_l if forward else far_s
        strip = along(-LONG if forward else SHORT) * 2 + core
        for j in (3, 2, 1):
            target = along(j if forward else -j)
            distance = held + j if forward else NZ - held - j
            for e in range(2):
                which = core if e == 0 else other
                picked[2 * (j - 1) + e] = normalized(buf[blk[strip, target * 2 + which]].astype(jnp.float32), gains[1])
                go(remote(
                    picked.at[2 * (j - 1) + e], x_ref.at[core, distance], far_send, far_recv,
                    {"img": img, "tile": target * 2 + which},
                ))

    def tick(i):
        if 1 <= i <= 8:
            unless_last(i, 1, whole(shards(1), zw_send, zw_recv.at[i - 1]).wait_recv)
        if i == 0:
            zw_start(1)
        if i <= 6:
            zw_start(i + 2)
        if 1 <= i <= 8:
            twin_start(i)
        if 2 <= i <= 9:
            unless_last(i - 1, 0, whole(shards(1), e_send, e_recv.at[i - 2]).wait_recv)
        if 1 <= i <= 9:
            x1_start(i - 1)
        if 2 <= i <= 10:
            whole(shards(2 * len(group(i - 2))), a_send, a_recv.at[i - 2]).wait_recv()
            x2_start(i - 2)
        if 3 <= i <= 11:
            whole(shards(len(group(i - 3))), a2_send, a2_recv.at[i - 3]).wait_recv()
            y_start(i - 3)
        if 5 <= i <= 5 + 8:
            count = len(group(i - 5))
            whole(w_ref.at[:, bp, :, pl.ds(0, count), core], b_send, b_recv.at[i - 5]).wait_recv()
            d2_start(i - 5)

    c_start(1, 0)
    tick(0)
    c_start(1, 1)
    for strip in range(NT):
        blk_rows[strip : strip + 1, :] = jnp.sum(
            jnp.where(reader_rows[...] == strip, pick_rows[...], 0), axis=0, keepdims=True
        )
    blk_copy = pltpu.make_async_copy(blk_rows, blk, blk_sem)
    blk_copy.start()

    tick(1)
    c_pass(1, 0)
    blk_copy.wait()
    for index, gain_ref in enumerate((fine_gain_ref, coarse_gain_ref)):
        gains[index] = gain_ref[...].reshape(1, D)
    share_step(0)
    tick(2)
    c_pass(1, 1)
    tick(3)
    c_pass(2, 0)
    share_step(1)
    tick(4)
    c_pass(2, 1)
    tick(5)
    c_pass(3, 0)
    share_step(2)
    tick(6)
    c_pass(3, 1)
    tick(7)
    c_pass(4, 0)
    share_step(3)
    tick(8)

    fine_copy.wait()
    whole(up_ref.at[pl.ds(0, 4)], up_send, up_recv).wait_recv()

    rows = lax.broadcasted_iota(jnp.int32, (32, BLOCK), 0) // 2
    spread = (rows == lax.broadcasted_iota(jnp.int32, (32, BLOCK), 1)).astype(jnp.bfloat16)

    def fine_norm(first, last):
        @pl.loop(first, last)
        def _(i):
            up = jnp.dot(spread, up_ref[i], preferred_element_type=jnp.float32)
            for half in range(2):
                part = pl.ds(pl.multiple_of(i * 64 + half * 32, 32), 32)
                hidden = fine[part, :].astype(jnp.float32) + up
                fine_n[part, :] = normalized(hidden, gains[0])

    def slab(index):
        return w_ref[index // 6, lax.rem(index // 3, 2), lax.rem(index, 3)].reshape(D, 128)

    def project_query():
        @pl.loop(0, 3)
        def _(j):
            pair = jnp.concatenate([slab(2 * j), slab(2 * j + 1)], axis=1)
            query[:, pl.ds(pl.multiple_of(j * 256, 256), 256)] = jnp.dot(
                fine_n[...], pair, preferred_element_type=jnp.float32
            ).astype(jnp.bfloat16)

    def order_out():
        @pl.loop(0, NZ)
        def _(k):
            part = pl.ds(pl.multiple_of(k * 48, 48), 48)
            for j in range(6):
                even = w_ref[3, j // 3, j % 3, k, 0].astype(jnp.float32)
                odd = w_ref[3, j // 3, j % 3, k, 1].astype(jnp.float32)
                for half in range(2):
                    cut = slice(24 * half, 24 * half + 24)
                    w_out[part, pl.ds((j + 6 * half) * 128, 128)] = jnp.concatenate(
                        [even[cut], odd[cut]], axis=0
                    ).astype(jnp.bfloat16)

    c_pass(4, 1)
    send_far(False)
    tick(9)
    fine_norm(0, 4)
    tick(10)
    c_pass(5, 0)
    tick(11)
    c_pass(5, 1)
    send_far(True)
    tick(12)
    share_step(4)
    share_step(5)
    tick(13)
    fine_norm(4, 8)
    whole(w_ref.at[:, :, :, :, core], d_send, d_recv).wait_recv()
    project_query()
    order_out()
    whole(x_ref.at[0, pl.ds(0, LONG + SHORT + 1)], near_send, near_recv).wait_recv()
    whole(x_ref.at[0, pl.ds(0, 12)], far_send, far_recv).wait_recv()

    @pl.loop(0, 16, unroll=4)
    def _(r):
        reader = readers_ref[r, tile]
        lane = lax.rem(reader, 2)
        distance = lax.rem((z - reader // 2) * (1 - 2 * lane) + NZ, NZ)
        coarse_n[pl.ds(pl.multiple_of(r * BLOCK, BLOCK), BLOCK), :] = x_ref[lane, distance]

    def projected(p):
        pair = jnp.concatenate([slab(6 + p), slab(12 + p)], axis=1)
        return jnp.dot(coarse_n[...], pair, preferred_element_type=jnp.float32).astype(jnp.bfloat16)

    low = lax.broadcasted_iota(jnp.int32, (1, 128), 1) < HDIM
    keyval[0] = projected(0)

    @pl.loop(0, HEADS // 2, unroll=6)
    def _(p):
        lanes = pl.ds(pl.multiple_of(p * 128, 128), 128)
        both = keyval[lax.rem(p, 2)]
        keyval[lax.rem(p + 1, 2)] = projected(jnp.minimum(p + 1, HEADS // 2 - 1))
        keys, values = both[:, :128], both[:, 128:]
        zero, one = jnp.zeros_like(keys), jnp.ones_like(values)
        key_pair = [jnp.where(low, keys, zero), jnp.where(low, zero, keys)]
        value_pair = [jnp.where(low, values, one), jnp.where(low, one, values)]
        queries = query[:, lanes]
        results = []
        for h in range(2):
            scores = lax.dot_general(
                queries, key_pair[h], (((1,), (1,)), ((), ())), preferred_element_type=jnp.float32
            )
            top = jnp.max(scores, axis=-1, keepdims=True)
            exponent = jnp.exp2((scores - top) * (HDIM ** (-0.5) * LOG2E)).astype(jnp.bfloat16)
            results.append(jnp.dot(exponent, value_pair[h], preferred_element_type=jnp.float32))
        total = pltpu.roll(jnp.where(low, results[1], results[0]), HDIM, 1)
        mixed[:, lanes] = (jnp.where(low, results[0], results[1]) / total).astype(jnp.bfloat16)

    drain()


def body(coarse, fine_embed, fine_gain, coarse_gain, w_query, w_kv, w_out, readers, picks):
    vmem, smem = pl.BlockSpec(memory_space=pltpu.VMEM), pl.BlockSpec(memory_space=pltpu.SMEM)
    hbm = pl.BlockSpec(memory_space=pl.ANY)
    bf16 = jnp.bfloat16
    strip = pltpu.VMEM((8, BLOCK, D), bf16)
    near = LONG + SHORT + 1

    dma = pltpu.SemaphoreType.DMA

    def many(count):
        return dma((count,))

    mixed, w_out_whole = pl.pallas_call(
        kernel,
        out_shape=(
            pltpu.VMEM((fine_embed.shape[0], HD), bf16), pltpu.VMEM((HD, D), bf16)
        ),
        in_specs=[vmem] * 4 + [smem, vmem, vmem] + [hbm, vmem, vmem],
        out_specs=(vmem, vmem),
        scratch_shapes=[
            pltpu.VMEM((4, 2, 3, NZ, 2, 48, 128), bf16),
            pltpu.VMEM((2, NZ, BLOCK, D), bf16),
            strip,
        ] + [strip] * (LONG + SHORT) + [
            pltpu.VMEM((near, BLOCK, D), bf16),
            pltpu.VMEM((6, BLOCK, D), bf16),
            pltpu.VMEM((6, BLOCK, D), bf16),
            pltpu.VMEM((512, D), bf16),
            pltpu.VMEM((512, D), bf16),
            pltpu.VMEM((256, D), bf16),
            pltpu.VMEM((512, HD), bf16),
            pltpu.VMEM((2, 256, 256), bf16),
            pltpu.VMEM((2, 1, D), jnp.float32),
            pltpu.VMEM((NT, NT), jnp.int32),
            pltpu.SMEM((NT, NT), jnp.int32),
            dma, dma,
            dma, many(8),
            dma, many(8),
            dma, many(2 * LONG),
            dma, dma,
            dma, dma,
            dma, dma,
            dma, many(9),
            dma, many(9),
            dma, many(9),
            dma, dma,
        ],
        compiler_params=pltpu.CompilerParams(
            collective_id=0, has_side_effects=True, vmem_limit_bytes=40 << 20
        ),
    )(*(pltpu.with_memory_space_constraint(operand, pltpu.HBM) for operand in (
        coarse.reshape(8, BLOCK, D), w_query, w_kv, w_out, readers.T, readers.T, picks.T, fine_embed, fine_gain,
        coarse_gain,
    )))
    return jnp.dot(mixed, w_out_whole, preferred_element_type=jnp.float32).astype(bf16)


def solution(mesh):
    placed = (
        P(("img", "tile"), None),
        P(("img", "tile"), None),
        P(),
        P(),
        P("tile", None),
        P("tile", None),
        P("tile", None),
        P("img", None),
        P("img", None),
    )
    return jax.shard_map(
        body, mesh=mesh, in_specs=placed, out_specs=P(("img", "tile"), None), check_vma=False
    )
```
